32 devices in a mesh: groups: 2 (over y), replica: 4 (over z), tensor: 4 (over x, core).
Axes of the slice: x: 2, y: 2, z: 4, core: 2. Of those that a mesh axis runs over, the one named last changes fastest.
Arguments:
- hidden: bfloat16 [64, 2, 8192], P(('groups', 'replica')), parts along dimension 0, may hold values from -6 to 6
- queries: bfloat16 [64, 2, 8192], P(('groups', 'replica'), None, 'tensor'), parts along dimension 0, may hold values from -60 to 60
- earlier_token_cache: bfloat16 [64, 2, 512, 1024], P(('groups', 'replica'), None, None, 'tensor'), parts along dimension 0, may hold values from -6 to 6
- lengths: int32 [8, 8], P(('groups', 'replica')), parts along dimension 0, may hold values from 1 to 3, 17 in all within a row
- request_hot_entry: int32 [64], P(('groups', 'replica')), parts along dimension 0, may hold values from 0 to 1
- destination: int32 [64], P(('groups', 'replica')), parts along dimension 0, may hold values from 0 to 3, as said below
- placement: int32 [4], P('groups'), parts along dimension 0, may hold values from 0 to 3
- base_key_value_weight: bfloat16 [8192, 2, 1024], P(None, None, 'tensor'), may hold values from -0.0625 to 0.0625
- adapter_first_factors: bfloat16 [4, 8192, 256], P('replica', 'tensor'), may hold values from -0.0625 to 0.0625
- adapter_second_factors: bfloat16 [4, 2, 128, 1024], P('replica', None, None, 'tensor'), may hold values from -0.5 to 0.5
Outputs:
- moved_cache: bfloat16 [64, 2, 512, 1024], P(('groups', 'replica'), None, None, 'tensor'), parts along dimension 0
- moved_attention: bfloat16 [64, 2, 8192], P(('groups', 'replica'), None, 'tensor'), parts along dimension 0
- resident_first_factors: bfloat16 [4, 8192, 256], P('groups', 'tensor'), parts along dimension 0
- resident_second_factors: bfloat16 [4, 2, 128, 1024], P('groups', None, None, 'tensor'), parts along dimension 0
The draws below stay inside these ranges and needn't reach their ends.
There are 2 independent parts, one for each index of `groups`. The reference program is written for one: setup_inputs(seed, part) draws one part's arguments, and reference() takes and returns one part's arrays. A program takes and returns all parts, laid end to end along the dimension named above; an argument that names none is the same for every part. Nothing has to cross between parts.
Inputs may be any that keep to these rules, and one draw needn't show every extreme that they name: Each replica's 8 lengths sum to 17 blocks, and one of them is 3. A request's adapter is placement[request_hot_entry]. `placement`: entries may repeat. `destination`: each replica's requests name any one replica at most 2 times, and one replica is named exactly 2 times by the requests of every replica.
All inputs are finite; a program needn't handle non-finite values.
Results may differ from the reference program's by a relative error of at most 0.0052.
Values may be sent and summed in bfloat16 or wider, within the bound.
No kernel may reach another device: no remote copies, remote signals or barrier semaphores. Data moves between devices by JAX's collectives and lax.ppermute only.
A program may use at most 128 MiB of HBM per device.

```python
import math
from functools import partial
import jax
import jax.numpy as jnp
import numpy as np
from jax import lax

MODEL_WIDTH = 8192
HQ = 64
KEY_VALUE_HEADS = 8
HEAD_WIDTH = 128
ADAPTER_RANK = 128
BLOCK = 128
MAXBLK = 4
HOT = 2
REQ_DEV = 8
CTX = 512
REQS = 32
ADAPTER_COUNT = 4
PAIR = 2
RECV = 8
N_REPLICA = 4


def draw_queries(key, part):
    key = jax.random.fold_in(key, 11)
    result = jax.random.truncated_normal(key, -6.0, 6.0, (REQS, 2, HQ * HEAD_WIDTH), jnp.float32)
    return result.astype(jnp.bfloat16)


def draw_earlier_token_cache(key, part):
    key = jax.random.fold_in(key, 23)
    array_extent = (REQS, 2, CTX, KEY_VALUE_HEADS * HEAD_WIDTH)
    result = jax.random.truncated_normal(key, -6.0, 6.0, array_extent, jnp.float32)
    return result.astype(jnp.bfloat16)


def draw_destination(key, part):
    key = jax.random.fold_in(key, 37)
    per_pair = max(1, REQ_DEV // N_REPLICA)
    picks = REQ_DEV // per_pair
    target = jax.random.randint(jax.random.fold_in(key, 1), (), 0, N_REPLICA)

    def one_replica(index):
        subkey = jax.random.fold_in(key, index + 2)
        chosen = jax.random.permutation(subkey, N_REPLICA)[:picks]
        holds = jnp.any(chosen == target)
        chosen = jnp.where(holds, chosen, chosen.at[0].set(target))
        spread = jnp.repeat(chosen, per_pair)
        shuffle = jax.random.permutation(jax.random.fold_in(subkey, 5), REQ_DEV)
        return spread[shuffle]
    return jax.vmap(one_replica)(jnp.arange(N_REPLICA)).reshape(REQS).astype(jnp.int32)


def set_ends(drawn, key, least, top_value):
    dims = drawn.shape
    index_at = [jax.random.randint(jax.random.fold_in(key, axis), (), 0, dims[axis]) for axis in range(len(dims))]
    drawn = drawn.at[tuple(index_at)].set(least)
    longest = dims.index(max(dims))
    index_at[longest] = (index_at[longest] + 1) % dims[longest]
    return drawn.at[tuple(index_at)].set(top_value)


def steps_of(stream_key, shape, cuts, least, largest):
    loudness, own = 1.0, jax.random.fold_in(stream_key, 6)
    for axis_at, blocks in cuts:
        steps = jnp.exp(jax.random.uniform(jax.random.fold_in(own, axis_at), (blocks,), jnp.float32, least / len(cuts), largest / len(cuts)))
        loudness = loudness * jnp.repeat(steps, shape[axis_at] // blocks).reshape([-1 if axis == axis_at else 1 for axis in range(len(shape))])
    return loudness


def split_up(amount, total, most, lean):
    portions = [(1 << 20) // math.isqrt(rank ** lean) + 1 for rank in range(2, amount + 1)]
    spare, given = total - most - (amount - 1), [1] * (amount - 1)
    while spare > 0:
        movable = [i for i in range(amount - 1) if given[i] < most]
        mass, left = sum([portions[i] for i in movable]), spare
        for i in movable:
            addition = min(most - given[i], max(1, left * portions[i] // mass), spare)
            given[i] = given[i] + addition
            spare = spare - addition
    return np.array([most] + given)


def ragged(rng, count, total, reach, skew):
    if count == 2:
        one = jax.random.randint(rng, (), max(1, total - reach), min(reach, total - 1) + 1)
        return jnp.stack([one, total - one])
    tallies = jnp.asarray(split_up(count, total, reach, skew), jnp.int32)
    pairs = (count - 1) // 2
    donor, taker = tallies[1:1 + 2 * pairs:2], tallies[2:2 + 2 * pairs:2]
    slack = jnp.minimum(donor - 1, reach - taker)
    passed = jax.random.randint(jax.random.fold_in(rng, 1), (pairs,), 0, 1 << 20) % (slack + 1)
    tallies = tallies.at[1:1 + 2 * pairs:2].set(donor - passed).at[2:2 + 2 * pairs:2].set(taker + passed)
    return tallies[jax.random.permutation(jax.random.fold_in(rng, 2), count)]


def centred(own_key, extent, scale, reach, pieces=(), kind=jnp.bfloat16):
    array = scale * jax.random.normal(own_key, extent, jnp.float32)
    if pieces:
        array = array * steps_of(own_key, extent, pieces, -0.22, 0.18)
    return jnp.clip(array, -reach, reach).astype(kind)


def setup_inputs(seed: int = 0, part: int = 0) -> dict:
    seeds = jax.random.split(jax.random.key(seed), 11)
    own_keys = jax.random.split(jax.random.fold_in(seeds[10], part), 11)
    hidden = centred(own_keys[0], (REQS, 2, MODEL_WIDTH), 1.0, 6.0, ((0, 4),))
    queries = draw_queries(jax.random.fold_in(jax.random.fold_in(seeds[10], part), 71), part)
    earlier_token_cache = draw_earlier_token_cache(jax.random.fold_in(jax.random.fold_in(seeds[10], part), 71), part)
    lengths = jax.vmap(lambda own: ragged(own, REQ_DEV, 2 * REQ_DEV + 1, MAXBLK - 1, 2))(jax.random.split(own_keys[3], N_REPLICA)).reshape((N_REPLICA, REQ_DEV)).astype(jnp.int32)
    request_hot_entry = set_ends(jax.random.randint(own_keys[4], (REQS,), 0, HOT), jax.random.fold_in(own_keys[4], 1), 0, HOT - 1).astype(jnp.int32)
    destination = draw_destination(jax.random.fold_in(jax.random.fold_in(seeds[10], part), 71), part)
    placement = jax.random.randint(own_keys[6], (HOT,), 0, ADAPTER_COUNT).astype(jnp.int32)
    base_key_value_weight = centred(seeds[7], (MODEL_WIDTH, 2, KEY_VALUE_HEADS * HEAD_WIDTH), MODEL_WIDTH ** -0.5, 0.0625, ((2, 4),))
    adapter_first_factors = centred(seeds[8], (ADAPTER_COUNT, MODEL_WIDTH, 2 * ADAPTER_RANK), MODEL_WIDTH ** -0.5, 0.0625, ((0, 4), (1, 4)))
    adapter_second_factors = centred(seeds[9], (ADAPTER_COUNT, 2, ADAPTER_RANK, KEY_VALUE_HEADS * HEAD_WIDTH), ADAPTER_RANK ** -0.5, 0.5, ((0, 4), (3, 4)))
    return {"hidden": hidden, "queries": queries, "earlier_token_cache": earlier_token_cache, "lengths": lengths, "request_hot_entry": request_hot_entry, "destination": destination, "placement": placement, "base_key_value_weight": base_key_value_weight, "adapter_first_factors": adapter_first_factors, "adapter_second_factors": adapter_second_factors}


def rotate_keys(key_rows, positions, head_size):
    half_size = head_size // 2
    frequency = 10000.0 ** (-(jnp.arange(half_size, dtype=jnp.float32) * 2.0 / head_size))
    angles = positions.astype(jnp.float32)[..., None] * frequency
    cosine_table = jnp.cos(angles)[..., None, :]
    sine_table = jnp.sin(angles)[..., None, :]
    first_half = key_rows[..., :half_size]
    second = key_rows[..., half_size:]
    return jnp.concatenate([first_half * cosine_table - second * sine_table, second * cosine_table + first_half * sine_table], -1)


def single_request(element_entry, placement, base_key_value_weight, adapter_first_factors, adapter_second_factors):
    tokens, query_rows, old_cache, block_count, hot_slot = element_entry
    adapter_index = placement[hot_slot].astype(jnp.int32)
    first_factor = lax.dynamic_index_in_dim(adapter_first_factors, adapter_index, 0, keepdims=False)
    second_factor = lax.dynamic_index_in_dim(adapter_second_factors, adapter_index, 0, keepdims=False)
    key_width = KEY_VALUE_HEADS * HEAD_WIDTH
    base_proj = jnp.dot(tokens, base_key_value_weight.reshape(MODEL_WIDTH, 2 * key_width), preferred_element_type=jnp.float32)
    low_rank = jnp.dot(tokens, first_factor, preferred_element_type=jnp.float32).astype(jnp.bfloat16)
    delta_key = jnp.dot(low_rank[:, :ADAPTER_RANK], second_factor[0], preferred_element_type=jnp.float32)
    delta_value = jnp.dot(low_rank[:, ADAPTER_RANK:], second_factor[1], preferred_element_type=jnp.float32)
    key_pre = (base_proj[:, :key_width] + delta_key).reshape(2, KEY_VALUE_HEADS, HEAD_WIDTH)
    write_start = (BLOCK * block_count).astype(jnp.int32)
    positions = write_start + jnp.arange(2, dtype=jnp.int32)
    new_key = rotate_keys(key_pre, positions, HEAD_WIDTH).reshape(2, key_width).astype(jnp.bfloat16)
    new_value = (base_proj[:, key_width:] + delta_value).astype(jnp.bfloat16)
    fresh_rows = jnp.stack([new_key, new_value])
    row_index = jnp.arange(CTX, dtype=jnp.int32)
    kept = jnp.where((row_index < write_start)[None, :, None], old_cache, jnp.zeros_like(old_cache))
    written = lax.dynamic_update_slice(kept, fresh_rows, (jnp.int32(0), write_start, jnp.int32(0)))
    group_size = HQ // KEY_VALUE_HEADS
    query_f = query_rows.astype(jnp.float32).reshape(2, KEY_VALUE_HEADS, group_size, HEAD_WIDTH)
    key_f = written[0].astype(jnp.float32).reshape(CTX, KEY_VALUE_HEADS, HEAD_WIDTH)
    value_f = written[1].astype(jnp.float32).reshape(CTX, KEY_VALUE_HEADS, HEAD_WIDTH)
    scores = jnp.einsum("tgjd,pgd->tgjp", query_f, key_f) * (HEAD_WIDTH ** -0.5)
    last_allowed = positions
    allowed = row_index[None, :] <= last_allowed[:, None]
    scores = jnp.where(allowed[:, None, None, :], scores, -1e30)
    row_max = jnp.max(scores, -1, keepdims=True)
    weights = jnp.exp(scores - row_max)
    probabilities = (weights / jnp.sum(weights, -1, keepdims=True)).astype(jnp.bfloat16)
    attended = jnp.einsum("tgjp,pgd->tgjd", probabilities.astype(jnp.float32), value_f)
    return written, attended.astype(jnp.bfloat16).reshape(2, HQ * HEAD_WIDTH)


def reference(hidden, queries, earlier_token_cache, lengths, request_hot_entry, destination, placement, base_key_value_weight, adapter_first_factors, adapter_second_factors):
    block_counts = lengths.reshape(-1)
    replica_worker = partial(single_request, placement=placement, base_key_value_weight=base_key_value_weight, adapter_first_factors=adapter_first_factors, adapter_second_factors=adapter_second_factors)
    written, attended = lax.map(replica_worker, (hidden, queries, earlier_token_cache, block_counts, request_hot_entry))
    target_grid = destination.reshape(N_REPLICA, REQ_DEV)
    request_order = jnp.arange(REQ_DEV, dtype=jnp.int32)
    same_target = target_grid[:, :, None] == target_grid[:, None, :]
    arrival = jnp.sum((same_target & (request_order[None, None, :] < request_order[None, :, None])).astype(jnp.int32), -1)
    sources = jnp.arange(N_REPLICA, dtype=jnp.int32)[:, None]
    target_slot = (target_grid * RECV + sources * PAIR + arrival).reshape(-1).astype(jnp.int32)
    total_slots = N_REPLICA * RECV
    moved_cache = jnp.zeros((total_slots, 2, CTX, KEY_VALUE_HEADS * HEAD_WIDTH), jnp.bfloat16).at[target_slot].set(written)
    moved_attention = jnp.zeros((total_slots, 2, HQ * HEAD_WIDTH), jnp.bfloat16).at[target_slot].set(attended)
    resident_first_factors = adapter_first_factors[placement]
    resident_second_factors = adapter_second_factors[placement]
    return moved_cache, moved_attention, resident_first_factors, resident_second_factors
```

```python
import functools

import jax
import jax.numpy as jnp
from jax import lax
from jax.experimental import pallas as pl
from jax.experimental.pallas import tpu as pltpu
from jax.sharding import PartitionSpec as P

HEAD_WIDTH = 128
BLOCK = 128
TILE = 16
LANES = 128
SMEM = pl.BlockSpec(memory_space=pltpu.SMEM)
VMEM = pl.BlockSpec(memory_space=pltpu.VMEM)
ANY = pl.BlockSpec(memory_space=pl.ANY)


def exchange(values, axis, mask):
    size = lax.axis_size(axis)
    return lax.ppermute(values, axis, [(i, i ^ mask) for i in range(size)])


def run_copies(copies):
    for condition, copy in copies:
        pl.when(condition)(copy.start)
    for condition, copy in copies:
        pl.when(condition)(copy.wait)


def pack_kernel(patterns, live, me_ref, dest_ref, count_ref, cache_ref, *rest):
    outs, sems = rest[: len(patterns)], rest[len(patterns)]
    requests = dest_ref.shape[0]
    copies = []
    for pattern, out_ref in zip(patterns, outs):
        offset = jnp.int32(0)
        for r in range(requests):
            mine = dest_ref[r] == (me_ref[0] ^ pattern)
            blocks = count_ref[r]
            for b in range(live):
                copies.append(
                    (
                        mine & (b < blocks),
                        pltpu.make_async_copy(
                            cache_ref.at[r, :, pl.ds(b * BLOCK, BLOCK), :],
                            out_ref.at[jnp.minimum(offset + b, out_ref.shape[0] - 1)],
                            sems.at[len(copies)],
                        ),
                    )
                )
            offset = offset + jnp.where(mine, blocks, 0)
    run_copies(copies)


def pack(me, destination, counts, cache, patterns, cap):
    requests, _, context, width = cache.shape
    live = context // BLOCK - 1
    shape = jax.ShapeDtypeStruct((cap, 2, BLOCK, width), cache.dtype)
    return pl.pallas_call(
        functools.partial(pack_kernel, patterns, live),
        out_shape=[shape] * len(patterns),
        in_specs=[SMEM, SMEM, SMEM, ANY],
        out_specs=[ANY] * len(patterns),
        scratch_shapes=[pltpu.SemaphoreType.DMA((len(patterns) * requests * live,))],
        name="pack",
    )(me, destination, counts, cache)


def unpack_kernel(patterns, own, fill, tail, pairs, live, *refs):
    me_ref, dest_ref, count_ref = refs[:3]
    at = 3
    if own:
        cache_ref = refs[at]
        at += 1
    received = refs[at : at + len(patterns)]
    at += len(patterns)
    replicas, requests = dest_ref.shape
    if tail:
        smalls = refs[at : at + replicas]
        at += replicas
    if not fill:
        at += 1
    out_ref = refs[at]
    at += 1
    if tail:
        att_ref = refs[at]
        at += 1
    sems = refs[at]
    at += 1
    if fill:
        zero_ref = refs[at]
        at += 1
        zero_ref[...] = jnp.zeros_like(zero_ref)
    if tail:
        stage_ref = refs[at]
    width = out_ref.shape[3]
    me = me_ref[0]
    copies = []

    def add(condition, source, target):
        copies.append((condition, pltpu.make_async_copy(source, target, sems.at[len(copies)])))

    slot_info = []
    for pattern in range(replicas):
        source_replica = me ^ pattern
        arrived = jnp.int32(0)
        offset = jnp.int32(0)
        lengths_of = [jnp.int32(-1)] * pairs
        for r in range(requests):
            mine = dest_ref[pattern, r] == me
            blocks = count_ref[pattern, r]
            slot = source_replica * pairs + jnp.minimum(arrived, pairs - 1)
            for b in range(live):
                place = pl.ds(b * BLOCK, BLOCK)
                if pattern == 0 and own:
                    add(mine & (b < blocks), cache_ref.at[r, :, place, :], out_ref.at[slot, :, place, :])
                if pattern in patterns:
                    source_ref = received[patterns.index(pattern)]
                    position = jnp.minimum(offset + b, source_ref.shape[0] - 1)
                    add(mine & (b < blocks), source_ref.at[position], out_ref.at[slot, :, place, :])
            lengths_of = [
                jnp.where(mine & (arrived == k), blocks, lengths_of[k]) for k in range(pairs)
            ]
            arrived = arrived + jnp.where(mine, 1, 0)
            offset = offset + jnp.where(mine, blocks, 0)
        for k in range(pairs):
            slot_info.append((pattern, k, source_replica * pairs + k, lengths_of[k]))
    if fill:
        for pattern, k, slot, blocks in slot_info:
            for b in range(live + 1):
                add(b >= blocks, zero_ref, out_ref.at[slot, :, pl.ds(b * BLOCK, BLOCK), :])
    if tail:
        rows = lax.broadcasted_iota(jnp.int32, (TILE, LANES), 0)
        heads = width // LANES
        for index, (pattern, k, slot, blocks) in enumerate(slot_info):
            small = smalls[pattern][k]
            filled = blocks >= 0
            att_ref[slot] = jnp.where(filled, small[:, :width], jnp.zeros((), small.dtype))
            fresh = small[:, width:].astype(jnp.float32)
            for kv in range(2):
                for head in range(heads):
                    at_row = 2 * (kv * heads + head)
                    moved = pltpu.roll(fresh, (TILE - at_row) % TILE, 0)
                    stage_ref[index, kv, :, pl.ds(head * LANES, LANES)] = jnp.where(
                        rows < 2, moved, 0.0
                    ).astype(jnp.bfloat16)
            start = pl.multiple_of(jnp.maximum(blocks, 0) * BLOCK, BLOCK)
            add(filled, stage_ref.at[index], out_ref.at[slot, :, pl.ds(start, TILE), :])
    run_copies(copies)


def unpack(me, dest_all, count_all, cache, received, smalls, out, pairs, context):
    replicas, requests = dest_all.shape
    patterns = tuple(sorted(received))
    own, fill, tail = cache is not None, out is None, smalls is not None
    blocks_in = received[patterns[0]]
    width = blocks_in.shape[3]
    live = context // BLOCK - 1
    slots = replicas * pairs
    args, specs = [me, dest_all, count_all], [SMEM] * 3
    if own:
        args.append(cache)
        specs.append(ANY)
    for pattern in patterns:
        args.append(received[pattern])
        specs.append(ANY)
    if tail:
        args += list(smalls)
        specs += [VMEM] * len(smalls)
    aliases = {}
    if not fill:
        aliases = {len(args): 0}
        args.append(out)
        specs.append(ANY)
    out_shape = [jax.ShapeDtypeStruct((slots, 2, context, width), blocks_in.dtype)]
    out_specs = [ANY]
    amount = (len(patterns) + (1 if own else 0)) * requests * live
    scratch = []
    if fill:
        amount += slots * (live + 1)
        scratch.append(pltpu.VMEM((2, BLOCK, width), blocks_in.dtype))
    if tail:
        amount += slots
        out_shape.append(jax.ShapeDtypeStruct((slots, TILE, width), blocks_in.dtype))
        out_specs.append(VMEM)
        scratch.append(pltpu.VMEM((slots, 2, TILE, width), blocks_in.dtype))
    return pl.pallas_call(
        functools.partial(unpack_kernel, patterns, own, fill, tail, pairs, live),
        out_shape=out_shape,
        in_specs=specs,
        out_specs=out_specs,
        scratch_shapes=[pltpu.SemaphoreType.DMA((amount,))] + scratch,
        input_output_aliases=aliases,
        name="unpack_tail" if tail else "unpack",
    )(*args)


def select_kernel(half, extra, refs_in, *refs):
    me_ref, own_ref, other_ref, group_ref = refs[:4]
    pieces = refs[4 : 4 + refs_in]
    first_ref, second_ref, first_send_ref, second_send_ref, sems = refs[4 + refs_in :]
    hot = own_ref.shape[0]
    group = group_ref[0]
    copies = []

    def add(condition, source, target):
        copies.append((condition, pltpu.make_async_copy(source, target, sems.at[len(copies)])))

    for h in range(hot):
        for mask, piece in enumerate(pieces):
            other = (other_ref[h] ^ me_ref[0]) == mask
            add(other, piece.at[pl.ds(half, extra), :], second_send_ref.at[h])
            add(other, piece.at[pl.ds(0, half), :], first_send_ref.at[h])
            mine = (own_ref[h] ^ me_ref[0]) == mask
            add(mine, piece.at[pl.ds(half, extra), :], second_ref.at[h])
            start = pl.multiple_of(group * half, half)
            add(mine, piece.at[pl.ds(0, half), :], first_ref.at[h, pl.ds(start, half), :])
    run_copies(copies)


def select_hot(me, group, placement, other_placement, pieces, half, extra):
    hot = placement.shape[0]
    rank2 = pieces[0].shape[1]
    dtype = pieces[0].dtype
    return pl.pallas_call(
        functools.partial(select_kernel, half, extra, len(pieces)),
        out_shape=[
            jax.ShapeDtypeStruct((hot, 2 * half, rank2), dtype),
            jax.ShapeDtypeStruct((hot, extra, rank2), dtype),
            jax.ShapeDtypeStruct((hot, half, rank2), dtype),
            jax.ShapeDtypeStruct((hot, extra, rank2), dtype),
        ],
        in_specs=[SMEM] * 4 + [ANY] * len(pieces),
        out_specs=[ANY] * 4,
        scratch_shapes=[pltpu.SemaphoreType.DMA((4 * hot * len(pieces),))],
        name="select_hot",
    )(me, placement, other_placement, group, *pieces)


def place_kernel(group_ref, received_ref, _, out_ref, sem):
    half = received_ref.shape[1]
    start = pl.multiple_of((1 - group_ref[0]) * half, half)
    copy = pltpu.make_async_copy(received_ref, out_ref.at[:, pl.ds(start, half), :], sem)
    copy.start()
    copy.wait()


def place_half(group, received, out):
    return pl.pallas_call(
        place_kernel,
        out_shape=jax.ShapeDtypeStruct(out.shape, out.dtype),
        in_specs=[SMEM, ANY, ANY],
        out_specs=ANY,
        scratch_shapes=[pltpu.SemaphoreType.DMA],
        input_output_aliases={2: 0},
        name="place_half",
    )(group, received, out)


def rank_kernel(half, ids_ref, tokens_ref, me_ref, *refs):
    pieces, out_ref = refs[:-1], refs[-1]
    total = jnp.zeros(out_ref.shape, jnp.float32)
    for mask, piece in enumerate(pieces):
        product = jnp.dot(
            tokens_ref[...], piece[pl.ds(0, half), :], preferred_element_type=jnp.float32
        )
        total = total + jnp.where(ids_ref[...] == (me_ref[0] ^ mask), product, 0.0)
    out_ref[...] = total


def rank_products(ids, tokens, me, pieces, half):
    return pl.pallas_call(
        functools.partial(rank_kernel, half),
        out_shape=jax.ShapeDtypeStruct((tokens.shape[0], pieces[0].shape[1]), jnp.float32),
        in_specs=[VMEM, VMEM, SMEM] + [VMEM] * len(pieces),
        out_specs=VMEM,
        name="rank_products",
    )(ids, tokens, me, *pieces)


def attend_kernel(
    place_ref, count_ref, hot_ref, low_ref, second_ref, base_ref, cos_ref, sin_ref, query_ref,
    cache_ref, out_ref,
):
    r = pl.program_id(0)
    start = count_ref[r] * BLOCK
    entry = hot_ref[r]
    rank = second_ref.shape[2]
    width = cache_ref.shape[3]
    context = cache_ref.shape[2]
    heads = width // LANES
    low = low_ref[0]
    base = base_ref[0]
    delta_key = jnp.dot(low[:, :rank], second_ref[entry, 0], preferred_element_type=jnp.float32)
    delta_value = jnp.dot(low[:, rank:], second_ref[entry, 1], preferred_element_type=jnp.float32)
    key_pre = base[:, :width] + delta_key
    new_value = (base[:, width:] + delta_value).astype(jnp.bfloat16)
    columns = lax.broadcasted_iota(jnp.int32, (TILE, context), 1)
    second_token = lax.broadcasted_iota(jnp.int32, (TILE, 1), 0) >= TILE // 2
    fresh_keys, fresh_values = [], []
    for head in range(heads):
        lanes = slice(head * LANES, (head + 1) * LANES)
        k = key_pre[:, lanes]
        swapped = pltpu.roll(k, LANES // 2, 1)
        new_key = (k * cos_ref[0] + swapped * sin_ref[0]).astype(jnp.bfloat16).astype(jnp.float32)
        value_rows = new_value[:, lanes].astype(jnp.float32)
        fresh_keys.append(new_key)
        fresh_values.append(value_rows)
        q = query_ref[0, head]
        qf = q.astype(jnp.float32)
        scale = HEAD_WIDTH ** (-0.5)
        scores = lax.dot_general(
            q, cache_ref[0, 0, :, lanes], (((1,), (1,)), ((), ())),
            preferred_element_type=jnp.float32,
        ) * scale
        scores = jnp.where(columns < start, scores, -1e30)
        s0 = jnp.sum(qf * new_key[0:1], -1, keepdims=True) * scale
        s1 = jnp.sum(qf * new_key[1:2], -1, keepdims=True) * scale
        s1 = jnp.where(second_token, s1, -1e30)
        top = jnp.maximum(jnp.max(scores, -1, keepdims=True), jnp.maximum(s0, s1))
        weights = jnp.exp(scores - top)
        w0 = jnp.exp(s0 - top)
        w1 = jnp.exp(s1 - top)
        total = jnp.sum(weights, -1, keepdims=True) + w0 + w1
        probs = (weights / total).astype(jnp.bfloat16)
        p0 = (w0 / total).astype(jnp.bfloat16).astype(jnp.float32)
        p1 = (w1 / total).astype(jnp.bfloat16).astype(jnp.float32)
        attended = jnp.dot(
            probs, cache_ref[0, 1, :, lanes], preferred_element_type=jnp.float32
        )
        attended = attended + p0 * value_rows[0:1] + p1 * value_rows[1:2]
        out_ref[0, :, lanes] = attended.astype(jnp.bfloat16)
    fresh = fresh_keys + fresh_values
    if 2 * len(fresh) < TILE:
        fresh.append(jnp.zeros((TILE - 2 * len(fresh), LANES), jnp.float32))
    out_ref[0, :, width:] = jnp.concatenate(fresh, 0).astype(jnp.bfloat16)


def attend(place, counts, hot, low, second, base, cos, sin, query, cache, slots):
    requests, _, context, width = cache.shape
    heads = width // LANES

    def by_request(shape):
        return pl.BlockSpec((1,) + shape, lambda r, p, c, h: (r,) + (0,) * len(shape))

    return pl.pallas_call(
        attend_kernel,
        out_shape=jax.ShapeDtypeStruct((slots, TILE, width + LANES), cache.dtype),
        grid_spec=pltpu.PrefetchScalarGridSpec(
            num_scalar_prefetch=3,
            grid=(requests,),
            in_specs=[
                by_request((2, low.shape[2])),
                pl.BlockSpec(second.shape, lambda r, p, c, h: (0, 0, 0, 0)),
                by_request((2, 2 * width)),
                by_request((2, LANES)),
                by_request((2, LANES)),
                by_request((heads, TILE, LANES)),
                by_request((2, context, width)),
            ],
            out_specs=pl.BlockSpec((1, TILE, width + LANES), lambda r, p, c, h: (p[r], 0, 0)),
        ),
        name="attend",
    )(place, counts, hot, low, second, base, cos, sin, query, cache)


def per_device(
    hidden,
    queries,
    earlier_token_cache,
    lengths,
    request_hot_entry,
    destination,
    placement,
    base_key_value_weight,
    adapter_first_factors,
    adapter_second_factors,
):
    replicas = lax.axis_size("replica")
    tensor = lax.axis_size("tensor")
    replica = lax.axis_index("replica").astype(jnp.int32)
    group = lax.axis_index("groups").astype(jnp.int32)
    part = lax.axis_index("tensor").astype(jnp.int32)
    requests = hidden.shape[0]
    pairs = max(1, requests // replicas)
    context, width = earlier_token_cache.shape[2:]
    heads = width // LANES
    live = context // BLOCK - 1
    piece = adapter_first_factors.shape[1]
    half = piece // 2
    rank2 = adapter_first_factors.shape[2]
    rank = rank2 // 2
    hot = placement.shape[0]
    me = replica[None]
    group_at = group[None]
    counts = lengths.reshape(-1)

    first_half = lax.dynamic_slice_in_dim(adapter_first_factors[0], group * half, half, 0)
    second_half = lax.dynamic_index_in_dim(
        adapter_second_factors[0], group, 0, keepdims=False
    ).reshape(-1, rank2)
    extra = second_half.shape[0]
    info = jnp.concatenate([counts, destination]).astype(jnp.bfloat16)
    info = jnp.pad(info[None], ((0, TILE - 1), (0, rank2 - info.shape[0])))
    pieces = {0: jnp.concatenate([first_half, second_half, info], 0)}
    bit = replicas // 2
    while bit:
        for mask in list(pieces):
            pieces[mask ^ bit] = exchange(pieces[mask], "replica", bit)
        bit //= 2
    pieces = [pieces[mask] for mask in range(replicas)]
    infos = jnp.stack([p[half + extra, : 2 * requests] for p in pieces]).astype(jnp.int32)
    count_all, dest_all = infos[:, :requests], infos[:, requests:]

    cap = live * pairs
    patterns = tuple(range(1, replicas))
    packed = pack(me, destination, counts, earlier_token_cache, patterns, cap)
    received = {p: exchange(b, "replica", p) for p, b in zip(patterns, packed)}

    tokens = hidden.reshape(requests * 2, -1)
    ids = jnp.repeat(placement[request_hot_entry], 2)
    notes = jnp.concatenate(
        [ids[:, None], jnp.broadcast_to(placement[None], (requests * 2, hot))], 1
    ).astype(jnp.bfloat16)
    notes = jnp.pad(notes, ((0, 0), (0, LANES - 1 - hot)))
    theirs = lax.dynamic_slice_in_dim(tokens, part * piece + (1 - group) * half, half, 1)
    theirs = exchange(jnp.concatenate([theirs, notes], 1), "groups", 1)
    other_ids = theirs[:, half].astype(jnp.int32)
    other_placement = theirs[0, half + 1 : half + 1 + hot].astype(jnp.int32)
    ours = lax.dynamic_slice_in_dim(tokens, part * piece + group * half, half, 1)
    both = jnp.concatenate([ours, theirs[:, :half]], 0)
    both_ids = jnp.broadcast_to(
        jnp.concatenate([ids, other_ids])[:, None], (4 * requests, rank2)
    )
    products = rank_products(both_ids, both, me, pieces, half)
    low = products[: 2 * requests] + exchange(products[2 * requests :], "groups", 1)
    bit = 1
    while bit < tensor:
        low = low + exchange(low, "tensor", bit)
        bit *= 2
    low = low.astype(jnp.bfloat16).reshape(requests, 2, rank2)

    first, second, first_send, second_send = select_hot(
        me, group_at, placement, other_placement, pieces, half, extra
    )
    second_other = exchange(second_send, "groups", 1).reshape(hot, rank, width)
    second = second.reshape(hot, rank, width)
    resident_second = jnp.where(
        group == 0,
        jnp.stack([second, second_other], 1),
        jnp.stack([second_other, second], 1),
    )
    first_other = exchange(first_send, "groups", 1)
    resident_first = place_half(group_at, first_other, first)

    base = jnp.einsum(
        "ntd,dkc->ntkc", hidden, base_key_value_weight, preferred_element_type=jnp.float32
    ).reshape(requests, 2, 2 * width)
    positions = (BLOCK * counts)[:, None] + jnp.arange(2)[None, :]
    half_size = HEAD_WIDTH // 2
    frequency = 10000.0 ** (-(jnp.arange(half_size, dtype=jnp.float32) * 2.0 / HEAD_WIDTH))
    angles = positions.astype(jnp.float32)[..., None] * frequency
    cos, sin = jnp.cos(angles), jnp.sin(angles)
    cos = jnp.concatenate([cos, cos], -1)
    sin = jnp.concatenate([-sin, sin], -1)
    group_size = queries.shape[2] // width
    query = (
        queries.reshape(requests, 2, heads, group_size, HEAD_WIDTH)
        .transpose(0, 2, 1, 3, 4)
        .reshape(requests, heads, 2 * group_size, HEAD_WIDTH)
    )
    order = jnp.arange(requests)
    same = destination[:, None] == destination[None, :]
    arrival = jnp.sum((same & (order[None, :] < order[:, None])).astype(jnp.int32), 1)
    place = (destination ^ replica) * pairs + arrival
    small = attend(
        place, counts, request_hot_entry, low, resident_second, base, cos, sin, query,
        earlier_token_cache, replicas * pairs,
    ).reshape(replicas, pairs, TILE, width + LANES)
    smalls = [small[0]] + [exchange(small[p], "replica", p) for p in patterns]

    early = {1: received[1]}
    late = {p: received[p] for p in patterns if p != 1}
    (out,) = unpack(
        me, dest_all, count_all, earlier_token_cache, early, None, None, pairs, context
    )
    moved_cache, attended = unpack(
        me, dest_all, count_all, None, late, smalls, out, pairs, context
    )
    slots = replicas * pairs
    moved_attention = (
        attended.reshape(slots, 2, group_size, heads, HEAD_WIDTH)
        .transpose(0, 1, 3, 2, 4)
        .reshape(slots, 2, group_size * width)
    )
    return (moved_cache, moved_attention, resident_first, resident_second)


def solution(mesh):
    in_specs = (
        P(("groups", "replica"), None, None),
        P(("groups", "replica"), None, "tensor"),
        P(("groups", "replica"), None, None, "tensor"),
        P(("groups", "replica"), None),
        P(("groups", "replica")),
        P(("groups", "replica")),
        P("groups"),
        P(None, None, "tensor"),
        P("replica", "tensor", None),
        P("replica", None, None, "tensor"),
    )
    out_specs = (
        P(("groups", "replica"), None, None, "tensor"),
        P(("groups", "replica"), None, "tensor"),
        P("groups", "tensor", None),
        P("groups", None, None, "tensor"),
    )
    return jax.shard_map(
        per_device, mesh=mesh, in_specs=in_specs, out_specs=out_specs, check_vma=False
    )
```

```python
import functools

import jax
import jax.numpy as jnp
from jax import lax
from jax.experimental import pallas as pl
from jax.experimental.pallas import tpu as pltpu
from jax.sharding import PartitionSpec as P

HEAD_WIDTH = 128
BLOCK = 128
TILE = 16
LANES = 128
SMEM = pl.BlockSpec(memory_space=pltpu.SMEM)
VMEM = pl.BlockSpec(memory_space=pltpu.VMEM)
CHEAP = pl.CostEstimate(flops=1, bytes_accessed=1, transcendentals=0)
HBM = pl.BlockSpec(memory_space=pltpu.HBM)


def exchange(values, axis, mask):
    size = lax.axis_size(axis)
    return lax.ppermute(values, axis, [(i, i ^ mask) for i in range(size)])


def gate_kernel(*refs):
    pass


def gate(values, *after):
    return pl.pallas_call(
        gate_kernel,
        out_shape=[jax.ShapeDtypeStruct(v.shape, v.dtype) for v in values],
        in_specs=[HBM] * (len(values) + len(after)),
        out_specs=[HBM] * len(values),
        input_output_aliases={i: i for i in range(len(values))},
        cost_estimate=CHEAP,
        name="gate",
    )(*values, *after)


def pack_kernel(layout, live, me_ref, dest_ref, count_ref, cache_ref, *rest):
    outs = rest[: len(layout)]
    mark_ref, stage, in_sems, out_sems = rest[len(layout) :]
    mark_ref[...] = jnp.zeros_like(mark_ref)
    requests = dest_ref.shape[0]
    me = me_ref[0]
    moves = []
    for r in range(requests):
        blocks, target = count_ref[r], dest_ref[r]
        offset = jnp.int32(0)
        for earlier in range(r):
            offset = offset + jnp.where(dest_ref[earlier] == target, count_ref[earlier], 0)
        for b in range(live):
            index = r * live + b
            going = (b < blocks) & (target != me)
            position = offset + b
            inward = pltpu.make_async_copy(
                cache_ref.at[r, :, pl.ds(b * BLOCK, BLOCK), :], stage.at[index], in_sems.at[index]
            )
            outward = []
            for (pattern, first, amount), out_ref in zip(layout, outs):
                here = position - first
                outward.append(
                    (
                        going & (target == (me ^ pattern)) & (here >= 0) & (here < amount),
                        pltpu.make_async_copy(
                            stage.at[index],
                            out_ref.at[jnp.clip(here, 0, amount - 1)],
                            out_sems.at[index],
                        ),
                    )
                )
            moves.append((going, inward, outward))
    for going, inward, _ in moves:
        pl.when(going)(inward.start)
    for going, inward, outward in moves:
        pl.when(going)(inward.wait)
        for this, copy in outward:
            pl.when(this)(copy.start)
    for going, _, outward in moves:
        pl.when(going)(outward[0][1].wait)


def pack(me, destination, counts, cache, layout):
    requests, _, context, width = cache.shape
    live = context // BLOCK - 1
    return pl.pallas_call(
        functools.partial(pack_kernel, layout, live),
        out_shape=[
            jax.ShapeDtypeStruct((amount, 2, BLOCK, width), cache.dtype)
            for _, _, amount in layout
        ]
        + [jax.ShapeDtypeStruct((8, LANES), jnp.float32)],
        in_specs=[SMEM, SMEM, SMEM, HBM],
        out_specs=[HBM] * len(layout) + [VMEM],
        scratch_shapes=[
            pltpu.VMEM((requests * live, 2, BLOCK, width), cache.dtype),
            pltpu.SemaphoreType.DMA((requests * live,)),
            pltpu.SemaphoreType.DMA((requests * live,)),
        ],
        compiler_params=pltpu.CompilerParams(vmem_limit_bytes=60 << 20),
        cost_estimate=CHEAP,
        name="pack",
    )(me, destination, counts, cache)


def unpack_kernel(layout, own, fill, tail, pairs, live, *refs):
    me_ref, dest_ref, count_ref = refs[:3]
    at = 3
    if own:
        cache_ref = refs[at]
        at += 1
    received = refs[at : at + len(layout)]
    at += len(layout)
    replicas, requests = dest_ref.shape
    if tail:
        small_ref = refs[at]
        at += 1
    if not fill:
        at += 2
    out_ref = refs[at]
    at += 1
    if tail:
        att_ref = refs[at]
        at += 1
    sems = refs[at]
    at += 1
    if own:
        own_stage, own_sems = refs[at : at + 2]
        at += 2
    if fill:
        zero_ref = refs[at]
        at += 1
        zero_ref[...] = jnp.zeros_like(zero_ref)
    if tail:
        stage_ref = refs[at]
    width = out_ref.shape[3]
    me = me_ref[0]
    copies, moves = [], []
    used = 0

    def copy_to(source, target):
        nonlocal used
        used += 1
        return pltpu.make_async_copy(source, target, sems.at[used - 1])

    slot_info = []
    for pattern in range(replicas):
        source_replica = me ^ pattern
        arrived = jnp.int32(0)
        offset = jnp.int32(0)
        lengths_of = [jnp.int32(-1)] * pairs
        for r in range(requests):
            mine = dest_ref[pattern, r] == me
            blocks = count_ref[pattern, r]
            slot = source_replica * pairs + jnp.minimum(arrived, pairs - 1)
            for b in range(live):
                place = pl.ds(b * BLOCK, BLOCK)
                target = out_ref.at[slot, :, place, :]
                valid = mine & (b < blocks)
                if pattern == 0 and own:
                    index = r * live + b
                    inward = pltpu.make_async_copy(
                        cache_ref.at[r, :, place, :], own_stage.at[index], own_sems.at[index]
                    )
                    moves.append((valid, inward, [(valid, copy_to(own_stage.at[index], target))]))
                for (of, first, amount), received_ref in zip(layout, received):
                    if of == pattern:
                        here = offset + b - first
                        source = received_ref.at[jnp.clip(here, 0, amount - 1)]
                        inside = valid & (here >= 0) & (here < amount)
                        copies.append((inside, copy_to(source, target)))
            lengths_of = [
                jnp.where(mine & (arrived == k), blocks, lengths_of[k]) for k in range(pairs)
            ]
            arrived = arrived + jnp.where(mine, 1, 0)
            offset = offset + jnp.where(mine, blocks, 0)
        for k in range(pairs):
            slot_info.append((pattern, k, source_replica * pairs + k, lengths_of[k]))
    if fill:
        for pattern, k, slot, blocks in slot_info:
            for b in range(live + 1):
                target = out_ref.at[slot, :, pl.ds(b * BLOCK, BLOCK), :]
                copies.append((b >= blocks, copy_to(zero_ref, target)))
    for condition, inward, _ in moves:
        pl.when(condition)(inward.start)
    for condition, copy in copies:
        pl.when(condition)(copy.start)
    if tail:
        rows = lax.broadcasted_iota(jnp.int32, (TILE, LANES), 0)
        heads = width // LANES
        for index, (pattern, k, slot, blocks) in enumerate(slot_info):
            small = small_ref[me ^ pattern, k]
            filled = blocks >= 0
            att_ref[slot] = jnp.where(filled, small[:, :width], jnp.zeros((), small.dtype))
            fresh = small[:, width:].astype(jnp.float32)
            for kv in range(2):
                for head in range(heads):
                    at_row = 2 * (kv * heads + head)
                    moved = pltpu.roll(fresh, (TILE - at_row) % TILE, 0)
                    stage_ref[index, kv, :, pl.ds(head * LANES, LANES)] = jnp.where(
                        rows < 2, moved, 0.0
                    ).astype(jnp.bfloat16)
            start = pl.multiple_of(jnp.maximum(blocks, 0) * BLOCK, BLOCK)
            copy = copy_to(stage_ref.at[index], out_ref.at[slot, :, pl.ds(start, TILE), :])
            pl.when(filled)(copy.start)
            copies.append((filled, copy))
    for condition, inward, outward in moves:
        pl.when(condition)(inward.wait)
        for going, copy in outward:
            pl.when(going)(copy.start)
            copies.append((going, copy))
    for condition, copy in copies:
        pl.when(condition)(copy.wait)


def unpack(me, dest_all, count_all, cache, received, smalls, out, pairs, context, after):
    replicas, requests = dest_all.shape
    own, fill, tail = cache is not None, out is None, smalls is not None
    layout = tuple(sorted(received))
    like = cache if own else received[layout[0]]
    dtype, width = like.dtype, like.shape[-1]
    live = context // BLOCK - 1
    slots = replicas * pairs
    args, specs = [me, dest_all, count_all], [SMEM] * 3
    if own:
        args.append(cache)
        specs.append(HBM)
    for part in layout:
        args.append(received[part])
        specs.append(VMEM)
    if tail:
        args.append(smalls)
        specs.append(VMEM)
    aliases = {}
    if not fill:
        aliases = {len(args): 0}
        args += [out, after]
        specs += [HBM] * 2
    out_shape = [jax.ShapeDtypeStruct((slots, 2, context, width), dtype)]
    out_specs = [HBM]
    amount = (len(layout) + (1 if own else 0)) * requests * live
    scratch = []
    if own:
        scratch.append(pltpu.VMEM((requests * live, 2, BLOCK, width), dtype))
        scratch.append(pltpu.SemaphoreType.DMA((requests * live,)))
    if fill:
        amount += slots * (live + 1)
        scratch.append(pltpu.VMEM((2, BLOCK, width), dtype))
    if tail:
        amount += slots
        out_shape.append(jax.ShapeDtypeStruct((slots, TILE, width), dtype))
        out_specs.append(VMEM)
        scratch.append(pltpu.VMEM((slots, 2, TILE, width), dtype))
    return pl.pallas_call(
        functools.partial(unpack_kernel, layout, own, fill, tail, pairs, live),
        out_shape=out_shape,
        in_specs=specs,
        out_specs=out_specs,
        scratch_shapes=[pltpu.SemaphoreType.DMA((amount,))] + scratch,
        input_output_aliases=aliases,
        compiler_params=pltpu.CompilerParams(vmem_limit_bytes=60 << 20),
        cost_estimate=CHEAP,
        name="unpack_tail" if tail else "unpack",
    )(*args)


def adapt_kernel(half, extra, amount, me_ref, own_ref, other_ref, group_ref, ids_ref, tokens_ref, *refs):
    pieces = refs[:amount]
    first_ref, second_ref, first_send_ref, second_send_ref, product_ref, sems = refs[amount + 1 :]
    me, group = me_ref[0], group_ref[0]
    copies = []

    def add(condition, source, target):
        copies.append((condition, pltpu.make_async_copy(source, target, sems.at[len(copies)])))

    for h in range(own_ref.shape[0]):
        for mask, piece in enumerate(pieces):
            other = (other_ref[h] ^ me) == mask
            add(other, piece.at[pl.ds(half, extra), :], second_send_ref.at[h])
            add(other, piece.at[pl.ds(0, half), :], first_send_ref.at[h])
            mine = (own_ref[h] ^ me) == mask
            add(mine, piece.at[pl.ds(half, extra), :], second_ref.at[h])
            start = pl.multiple_of(group * half, half)
            add(mine, piece.at[pl.ds(0, half), :], first_ref.at[h, pl.ds(start, half), :])
    for condition, copy in copies:
        pl.when(condition)(copy.start)
    total = jnp.zeros(product_ref.shape, jnp.float32)
    for mask, piece in enumerate(pieces):
        product = jnp.dot(
            tokens_ref[...], piece[pl.ds(0, half), :], preferred_element_type=jnp.float32
        )
        total = total + jnp.where(ids_ref[...] == (me ^ mask), product, 0.0)
    product_ref[...] = total
    for condition, copy in copies:
        pl.when(condition)(copy.wait)


def adapt(me, group, placement, other_placement, ids, tokens, pieces, half, extra, after):
    hot = placement.shape[0]
    rank2 = pieces[0].shape[1]
    dtype = pieces[0].dtype
    return pl.pallas_call(
        functools.partial(adapt_kernel, half, extra, len(pieces)),
        out_shape=[
            jax.ShapeDtypeStruct((hot, 2 * half, rank2), dtype),
            jax.ShapeDtypeStruct((hot, extra, rank2), dtype),
            jax.ShapeDtypeStruct((hot, half, rank2), dtype),
            jax.ShapeDtypeStruct((hot, extra, rank2), dtype),
            jax.ShapeDtypeStruct((tokens.shape[0], rank2), jnp.float32),
        ],
        in_specs=[SMEM] * 4 + [VMEM] * (2 + len(pieces)) + [HBM],
        out_specs=[HBM] * 4 + [VMEM],
        scratch_shapes=[pltpu.SemaphoreType.DMA((4 * hot * len(pieces),))],
        compiler_params=pltpu.CompilerParams(vmem_limit_bytes=60 << 20),
        cost_estimate=CHEAP,
        name="adapt",
    )(me, placement, other_placement, group, ids, tokens, *pieces, after)


def place_kernel(group_ref, received_ref, _, out_ref, sem):
    half = received_ref.shape[1]
    start = pl.multiple_of((1 - group_ref[0]) * half, half)
    copy = pltpu.make_async_copy(received_ref, out_ref.at[:, pl.ds(start, half), :], sem)
    copy.start()
    copy.wait()


def place_half(group, received, out):
    return pl.pallas_call(
        place_kernel,
        out_shape=jax.ShapeDtypeStruct(out.shape, out.dtype),
        in_specs=[SMEM, VMEM, HBM],
        out_specs=HBM,
        scratch_shapes=[pltpu.SemaphoreType.DMA],
        compiler_params=pltpu.CompilerParams(vmem_limit_bytes=60 << 20),
        input_output_aliases={2: 0},
        cost_estimate=CHEAP,
        name="place_half",
    )(group, received, out)


def attend_kernel(
    place_ref, count_ref, hot_ref, low_ref, second_ref, base_ref, cos_ref, sin_ref, query_ref,
    cache_ref, _, out_ref,
):
    r = pl.program_id(0)
    start = count_ref[r] * BLOCK
    entry = hot_ref[r]
    rank = second_ref.shape[2]
    width = cache_ref.shape[3]
    context = cache_ref.shape[2]
    heads = width // LANES
    low = low_ref[0]
    base = base_ref[0]
    delta_key = jnp.dot(low[:, :rank], second_ref[entry, 0], preferred_element_type=jnp.float32)
    delta_value = jnp.dot(low[:, rank:], second_ref[entry, 1], preferred_element_type=jnp.float32)
    key_pre = base[:, :width] + delta_key
    new_value = (base[:, width:] + delta_value).astype(jnp.bfloat16)
    columns = lax.broadcasted_iota(jnp.int32, (TILE, context), 1)
    second_token = lax.broadcasted_iota(jnp.int32, (TILE, 1), 0) >= TILE // 2
    fresh_keys, fresh_values = [], []
    for head in range(heads):
        lanes = slice(head * LANES, (head + 1) * LANES)
        k = key_pre[:, lanes]
        swapped = pltpu.roll(k, LANES // 2, 1)
        new_key = (k * cos_ref[0] + swapped * sin_ref[0]).astype(jnp.bfloat16).astype(jnp.float32)
        value_rows = new_value[:, lanes].astype(jnp.float32)
        fresh_keys.append(new_key)
        fresh_values.append(value_rows)
        q = query_ref[0, head]
        qf = q.astype(jnp.float32)
        scale = HEAD_WIDTH ** (-0.5)
        scores = lax.dot_general(
            q, cache_ref[0, 0, :, lanes], (((1,), (1,)), ((), ())),
            preferred_element_type=jnp.float32,
        ) * scale
        scores = jnp.where(columns < start, scores, -1e30)
        s0 = jnp.sum(qf * new_key[0:1], -1, keepdims=True) * scale
        s1 = jnp.sum(qf * new_key[1:2], -1, keepdims=True) * scale
        s1 = jnp.where(second_token, s1, -1e30)
        top = jnp.maximum(jnp.max(scores, -1, keepdims=True), jnp.maximum(s0, s1))
        weights = jnp.exp(scores - top)
        w0 = jnp.exp(s0 - top)
        w1 = jnp.exp(s1 - top)
        total = jnp.sum(weights, -1, keepdims=True) + w0 + w1
        probs = (weights / total).astype(jnp.bfloat16)
        p0 = (w0 / total).astype(jnp.bfloat16).astype(jnp.float32)
        p1 = (w1 / total).astype(jnp.bfloat16).astype(jnp.float32)
        attended = jnp.dot(
            probs, cache_ref[0, 1, :, lanes], preferred_element_type=jnp.float32
        )
        attended = attended + p0 * value_rows[0:1] + p1 * value_rows[1:2]
        out_ref[0, :, lanes] = attended.astype(jnp.bfloat16)
    fresh = fresh_keys + fresh_values
    if 2 * len(fresh) < TILE:
        fresh.append(jnp.zeros((TILE - 2 * len(fresh), LANES), jnp.float32))
    out_ref[0, :, width:] = jnp.concatenate(fresh, 0).astype(jnp.bfloat16)


def attend(place, counts, hot, low, second, base, cos, sin, query, cache, slots, after):
    requests, _, context, width = cache.shape
    heads = width // LANES

    def by_request(shape):
        return pl.BlockSpec((1,) + shape, lambda r, p, c, h: (r,) + (0,) * len(shape))

    return pl.pallas_call(
        attend_kernel,
        out_shape=jax.ShapeDtypeStruct((slots, TILE, width + LANES), cache.dtype),
        grid_spec=pltpu.PrefetchScalarGridSpec(
            num_scalar_prefetch=3,
            grid=(requests,),
            in_specs=[
                by_request((2, low.shape[2])),
                pl.BlockSpec(second.shape, lambda r, p, c, h: (0, 0, 0, 0)),
                by_request((2, 2 * width)),
                by_request((2, LANES)),
                by_request((2, LANES)),
                by_request((heads, TILE, LANES)),
                by_request((2, context, width)),
                HBM,
            ],
            out_specs=pl.BlockSpec((1, TILE, width + LANES), lambda r, p, c, h: (p[r], 0, 0)),
        ),
        cost_estimate=CHEAP,
        name="attend",
    )(place, counts, hot, low, second, base, cos, sin, query, cache, after)


def per_device(
    hidden,
    queries,
    earlier_token_cache,
    lengths,
    request_hot_entry,
    destination,
    placement,
    base_key_value_weight,
    adapter_first_factors,
    adapter_second_factors,
):
    replicas = lax.axis_size("replica")
    tensor = lax.axis_size("tensor")
    replica = lax.axis_index("replica").astype(jnp.int32)
    group = lax.axis_index("groups").astype(jnp.int32)
    part = lax.axis_index("tensor").astype(jnp.int32)
    requests = hidden.shape[0]
    pairs = max(1, requests // replicas)
    context, width = earlier_token_cache.shape[2:]
    heads = width // LANES
    live = context // BLOCK - 1
    piece = adapter_first_factors.shape[1]
    half = piece // 2
    rank2 = adapter_first_factors.shape[2]
    rank = rank2 // 2
    hot = placement.shape[0]
    me = replica[None]
    group_at = group[None]
    counts = lengths.reshape(-1)

    first_half = lax.dynamic_slice_in_dim(adapter_first_factors[0], group * half, half, 0)
    second_half = lax.dynamic_index_in_dim(
        adapter_second_factors[0], group, 0, keepdims=False
    ).reshape(-1, rank2)
    extra = second_half.shape[0]
    info = jnp.concatenate([counts, destination]).astype(jnp.bfloat16)
    info = jnp.pad(info[None], ((0, TILE - 1), (0, rank2 - info.shape[0])))
    pieces = {0: jnp.concatenate([first_half, second_half, info], 0)}
    bit = replicas // 2
    while bit:
        for mask in list(pieces):
            pieces[mask ^ bit] = exchange(pieces[mask], "replica", bit)
        bit //= 2
    pieces = [pieces[mask] for mask in range(replicas)]
    infos = jnp.stack([p[half + extra, : 2 * requests] for p in pieces]).astype(jnp.int32)
    count_all, dest_all = infos[:, :requests], infos[:, requests:]

    cap = live * pairs
    patterns = tuple(range(1, replicas))
    layout = tuple((p, 0, cap) for p in patterns)
    *packed, mark = pack(me, destination, counts, earlier_token_cache, layout)
    packed = dict(zip(layout, packed))

    tokens = hidden.reshape(requests * 2, -1)
    ids = jnp.repeat(placement[request_hot_entry], 2)
    notes = jnp.concatenate(
        [ids[:, None], jnp.broadcast_to(placement[None], (requests * 2, hot))], 1
    ).astype(jnp.bfloat16)
    notes = jnp.pad(notes, ((0, 0), (0, LANES - 1 - hot)))
    theirs = lax.dynamic_slice_in_dim(tokens, part * piece + (1 - group) * half, half, 1)
    (theirs,) = gate([jnp.concatenate([theirs, notes], 1)], mark)
    theirs = exchange(theirs, "groups", 1)
    other_ids = theirs[:, half].astype(jnp.int32)
    other_placement = theirs[0, half + 1 : half + 1 + hot].astype(jnp.int32)
    ours = lax.dynamic_slice_in_dim(tokens, part * piece + group * half, half, 1)
    both = jnp.concatenate([ours, theirs[:, :half]], 0)
    both_ids = jnp.broadcast_to(
        jnp.concatenate([ids, other_ids])[:, None], (4 * requests, rank2)
    )
    base = jnp.einsum(
        "ntd,dkc->ntkc", hidden, base_key_value_weight, preferred_element_type=jnp.float32
    ).reshape(requests, 2, 2 * width)
    received = {}
    first_parts = layout
    ready = gate(
        [packed[part] for part in first_parts],
        pieces[replicas // 2], pieces[1], both, both_ids, base,
    )
    for part, values in zip(first_parts, ready):
        received[part] = exchange(values, "replica", part[0])
    always = counts[0] > 0

    positions = (BLOCK * counts)[:, None] + jnp.arange(2)[None, :]
    half_size = HEAD_WIDTH // 2
    frequency = 10000.0 ** (-(jnp.arange(half_size, dtype=jnp.float32) * 2.0 / HEAD_WIDTH))
    angles = positions.astype(jnp.float32)[..., None] * frequency
    cos, sin = jnp.cos(angles), jnp.sin(angles)
    cos = jnp.concatenate([cos, cos], -1)
    sin = jnp.concatenate([-sin, sin], -1)
    group_size = queries.shape[2] // width
    query = (
        queries.reshape(requests, 2, heads, group_size, HEAD_WIDTH)
        .transpose(0, 2, 1, 3, 4)
        .reshape(requests, heads, 2 * group_size, HEAD_WIDTH)
    )
    order = jnp.arange(requests)
    same = destination[:, None] == destination[None, :]
    arrival = jnp.sum((same & (order[None, :] < order[:, None])).astype(jnp.int32), 1)
    place = destination * pairs + arrival
    slots = replicas * pairs

    def serve():
        first, second, first_send, second_send, products = adapt(
            me, group_at, placement, other_placement, both_ids, both, pieces, half, extra, both
        )
        low = products[: 2 * requests] + exchange(products[2 * requests :], "groups", 1)
        second_other = exchange(second_send, "groups", 1)
        (first_send,) = gate([first_send], low, second_other)
        first_other = exchange(first_send, "groups", 1)
        resident_first = place_half(group_at, first_other, first)
        theirs = second_other.reshape(hot, rank, width)
        bit = 1
        while bit < tensor:
            low = low + exchange(low, "tensor", bit)
            bit *= 2
        low = low.astype(jnp.bfloat16).reshape(requests, 2, rank2)
        ours = second.reshape(hot, rank, width)
        resident = jnp.where(
            group == 0, jnp.stack([ours, theirs], 1), jnp.stack([theirs, ours], 1)
        )
        (out,) = unpack(
            me, dest_all, count_all, earlier_token_cache, {}, None, None, pairs, context, None
        )
        small = attend(
            place, counts, request_hot_entry, low, resident, base, cos, sin, query,
            earlier_token_cache, slots, out,
        )
        small = small.reshape(replicas, pairs, TILE, width + LANES)
        smalls = lax.all_to_all(small, "replica", 0, 0, tiled=True)
        return smalls, resident_first, resident, out

    def nothing():
        return (
            jnp.zeros((replicas, pairs, TILE, width + LANES), jnp.bfloat16),
            jnp.zeros((hot, piece, rank2), jnp.bfloat16),
            jnp.zeros((hot, 2, rank, width), jnp.bfloat16),
            jnp.zeros((slots, 2, context, width), jnp.bfloat16),
        )

    smalls, resident_first, resident_second, out = lax.cond(always, serve, nothing)
    moved_cache, attended = unpack(
        me, dest_all, count_all, None, received, smalls, out, pairs, context, resident_first
    )
    moved_attention = (
        attended.reshape(slots, 2, group_size, heads, HEAD_WIDTH)
        .transpose(0, 1, 3, 2, 4)
        .reshape(slots, 2, group_size * width)
    )
    return (moved_cache, moved_attention, resident_first, resident_second)


def solution(mesh):
    in_specs = (
        P(("groups", "replica"), None, None),
        P(("groups", "replica"), None, "tensor"),
        P(("groups", "replica"), None, None, "tensor"),
        P(("groups", "replica"), None),
        P(("groups", "replica")),
        P(("groups", "replica")),
        P("groups"),
        P(None, None, "tensor"),
        P("replica", "tensor", None),
        P("replica", None, None, "tensor"),
    )
    out_specs = (
        P(("groups", "replica"), None, None, "tensor"),
        P(("groups", "replica"), None, "tensor"),
        P("groups", "tensor", None),
        P("groups", None, None, "tensor"),
    )
    return jax.shard_map(
        per_device, mesh=mesh, in_specs=in_specs, out_specs=out_specs, check_vma=False
    )
```

```python
import functools
import math

import jax
import jax.numpy as jnp
from jax import lax
from jax.experimental import pallas as pl
from jax.experimental.pallas import tpu as pltpu
from jax.sharding import PartitionSpec as P

HEAD_WIDTH = 128
BLOCK = 128
TILE = 16
LANES = 128
SMEM = pl.BlockSpec(memory_space=pltpu.SMEM)
VMEM = pl.BlockSpec(memory_space=pltpu.VMEM)
CHEAP = pl.CostEstimate(flops=1, bytes_accessed=1, transcendentals=0)
HBM = pl.BlockSpec(memory_space=pltpu.HBM)


def exchange(values, axis, mask):
    size = lax.axis_size(axis)
    return lax.ppermute(values, axis, [(i, i ^ mask) for i in range(size)])


def gate_kernel(*refs):
    pass


def gate(values, *after):
    return pl.pallas_call(
        gate_kernel,
        out_shape=[jax.ShapeDtypeStruct(v.shape, v.dtype) for v in values],
        in_specs=[HBM] * (len(values) + len(after)),
        out_specs=[HBM] * len(values),
        input_output_aliases={i: i for i in range(len(values))},
        cost_estimate=CHEAP,
        name="gate",
    )(*values, *after)


def pack_kernel(layout, live, me_ref, dest_ref, count_ref, cache_ref, *rest):
    outs = rest[: len(layout)]
    mark_ref, stage, in_sems, out_sems = rest[len(layout) :]
    mark_ref[...] = jnp.zeros_like(mark_ref)
    requests = dest_ref.shape[0]
    me = me_ref[0]
    moves = []
    for r in range(requests):
        blocks, target = count_ref[r], dest_ref[r]
        offset = jnp.int32(0)
        for earlier in range(r):
            offset = offset + jnp.where(dest_ref[earlier] == target, count_ref[earlier], 0)
        for b in range(live):
            index = r * live + b
            going = (b < blocks) & (target != me)
            position = offset + b
            inward = pltpu.make_async_copy(
                cache_ref.at[r, :, pl.ds(b * BLOCK, BLOCK), :], stage.at[index], in_sems.at[index]
            )
            outward = []
            for (pattern, first, amount), out_ref in zip(layout, outs):
                here = position - first
                outward.append(
                    (
                        going & (target == (me ^ pattern)) & (here >= 0) & (here < amount),
                        pltpu.make_async_copy(
                            stage.at[index],
                            out_ref.at[jnp.clip(here, 0, amount - 1)],
                            out_sems.at[index],
                        ),
                    )
                )
            moves.append((going, inward, outward))
    for going, inward, _ in moves:
        pl.when(going)(inward.start)
    for going, inward, outward in moves:
        pl.when(going)(inward.wait)
        for this, copy in outward:
            pl.when(this)(copy.start)
    for going, _, outward in moves:
        pl.when(going)(outward[0][1].wait)


def pack(me, destination, counts, cache, layout):
    requests, _, context, width = cache.shape
    live = context // BLOCK - 1
    return pl.pallas_call(
        functools.partial(pack_kernel, layout, live),
        out_shape=[
            jax.ShapeDtypeStruct((amount, 2, BLOCK, width), cache.dtype)
            for _, _, amount in layout
        ]
        + [jax.ShapeDtypeStruct((8, LANES), jnp.float32)],
        in_specs=[SMEM, SMEM, SMEM, HBM],
        out_specs=[HBM] * len(layout) + [VMEM],
        scratch_shapes=[
            pltpu.VMEM((requests * live, 2, BLOCK, width), cache.dtype),
            pltpu.SemaphoreType.DMA((requests * live,)),
            pltpu.SemaphoreType.DMA((requests * live,)),
        ],
        compiler_params=pltpu.CompilerParams(vmem_limit_bytes=60 << 20),
        cost_estimate=CHEAP,
        name="pack",
    )(me, destination, counts, cache)


def unpack_kernel(layout, own, fill, tail, pairs, live, *refs):
    me_ref, dest_ref, count_ref = refs[:3]
    at = 3
    if own:
        cache_ref = refs[at]
        at += 1
    received = refs[at : at + len(layout)]
    at += len(layout)
    replicas, requests = dest_ref.shape
    if tail:
        small_ref = refs[at]
        at += 1
    at += 1 if fill else 2
    out_ref = refs[at]
    at += 1
    if tail:
        att_ref = refs[at]
        at += 1
    sems = refs[at]
    at += 1
    if own:
        own_stage, own_sems = refs[at : at + 2]
        at += 2
    if fill:
        zero_ref = refs[at]
        at += 1
        zero_ref[...] = jnp.zeros_like(zero_ref)
    if tail:
        stage_ref = refs[at]
    width = out_ref.shape[3]
    me = me_ref[0]
    copies, moves = [], []
    used = 0

    def copy_to(source, target):
        nonlocal used
        used += 1
        return pltpu.make_async_copy(source, target, sems.at[used - 1])

    slot_info = []
    used_patterns = {of for of, _, _ in layout} | ({0} if own else set())
    for pattern in range(replicas):
        if not (fill or tail or pattern in used_patterns):
            continue
        source_replica = me ^ pattern
        arrived = jnp.int32(0)
        lengths_of = [jnp.int32(-1)] * pairs
        which = [jnp.int32(0)] * pairs
        for r in range(requests):
            mine = dest_ref[pattern, r] == me
            blocks = count_ref[pattern, r]
            for k in range(pairs):
                this = mine & (arrived == k)
                lengths_of[k] = jnp.where(this, blocks, lengths_of[k])
                which[k] = jnp.where(this, r, which[k])
            arrived = arrived + jnp.where(mine, 1, 0)
        offset = jnp.int32(0)
        for k in range(pairs):
            blocks = lengths_of[k]
            slot = source_replica * pairs + k
            for b in range(live):
                place = pl.ds(b * BLOCK, BLOCK)
                target = out_ref.at[slot, :, place, :]
                valid = b < blocks
                if pattern == 0 and own:
                    index = k * live + b
                    inward = pltpu.make_async_copy(
                        cache_ref.at[which[k], :, place, :],
                        own_stage.at[index],
                        own_sems.at[index],
                    )
                    moves.append((valid, inward, [(valid, copy_to(own_stage.at[index], target))]))
                for (of, first, amount), received_ref in zip(layout, received):
                    if of == pattern:
                        here = offset + b - first
                        source = received_ref.at[jnp.clip(here, 0, amount - 1)]
                        inside = valid & (here >= 0) & (here < amount)
                        copies.append((inside, copy_to(source, target)))
            offset = offset + jnp.maximum(blocks, 0)
            slot_info.append((pattern, k, slot, blocks))
    if fill:
        for pattern, k, slot, blocks in slot_info:
            for b in range(live + 1):
                target = out_ref.at[slot, :, pl.ds(b * BLOCK, BLOCK), :]
                copies.append((b >= blocks, copy_to(zero_ref, target)))
    for condition, inward, _ in moves:
        pl.when(condition)(inward.start)
    for condition, copy in copies:
        pl.when(condition)(copy.start)
    if tail:
        columns = att_ref.shape[2]
        for index, (pattern, k, slot, blocks) in enumerate(slot_info):
            small = small_ref[me ^ pattern, k]
            filled = blocks >= 0
            att_ref[slot] = jnp.where(filled, small[:, :columns], jnp.zeros((), small.dtype))
            fresh = small[:, columns:].astype(jnp.float32)
            for kv in range(2):
                rows = fresh[:, kv * width : (kv + 1) * width]
                rows = jnp.concatenate([rows, jnp.zeros((TILE - 2, width), jnp.float32)], 0)
                stage_ref[index, kv] = rows.astype(jnp.bfloat16)
            start = pl.multiple_of(jnp.maximum(blocks, 0) * BLOCK, BLOCK)
            copy = copy_to(stage_ref.at[index], out_ref.at[slot, :, pl.ds(start, TILE), :])
            pl.when(filled)(copy.start)
            copies.append((filled, copy))
    for condition, inward, outward in moves:
        pl.when(condition)(inward.wait)
        for going, copy in outward:
            pl.when(going)(copy.start)
            copies.append((going, copy))
    for condition, copy in copies:
        pl.when(condition)(copy.wait)


def unpack(me, dest_all, count_all, cache, received, smalls, out, pairs, context, after):
    replicas, requests = dest_all.shape
    own, fill, tail = cache is not None, out is None, smalls is not None
    layout = tuple(sorted(received))
    like = cache if own else out
    dtype, width = like.dtype, like.shape[-1]
    live = context // BLOCK - 1
    slots = replicas * pairs
    args, specs = [me, dest_all, count_all], [SMEM] * 3
    if own:
        args.append(cache)
        specs.append(HBM)
    for part in layout:
        args.append(received[part])
        specs.append(VMEM)
    if tail:
        args.append(smalls)
        specs.append(VMEM)
    aliases = {}
    if not fill:
        aliases = {len(args): 0}
        args.append(out)
        specs.append(HBM)
    args.append(after)
    specs.append(HBM)
    out_shape = [jax.ShapeDtypeStruct((slots, 2, context, width), dtype)]
    out_specs = [HBM]
    amount = (len(layout) + (1 if own else 0)) * pairs * live
    scratch = []
    if own:
        scratch.append(pltpu.VMEM((pairs * live, 2, BLOCK, width), dtype))
        scratch.append(pltpu.SemaphoreType.DMA((pairs * live,)))
    if fill:
        amount += slots * (live + 1)
        scratch.append(pltpu.VMEM((2, BLOCK, width), dtype))
    if tail:
        amount += slots
        out_shape.append(jax.ShapeDtypeStruct((slots, 2, smalls.shape[3] - 2 * width), dtype))
        out_specs.append(VMEM)
        scratch.append(pltpu.VMEM((slots, 2, TILE, width), dtype))
    return pl.pallas_call(
        functools.partial(unpack_kernel, layout, own, fill, tail, pairs, live),
        out_shape=out_shape,
        in_specs=specs,
        out_specs=out_specs,
        scratch_shapes=[pltpu.SemaphoreType.DMA((amount,))] + scratch,
        input_output_aliases=aliases,
        compiler_params=pltpu.CompilerParams(vmem_limit_bytes=60 << 20),
        cost_estimate=CHEAP,
        name="unpack",
    )(*args)


def adapt_kernel(half, extra, amount, me_ref, own_ref, other_ref, group_ref, ids_ref, tokens_ref, *refs):
    pieces = refs[:amount]
    first_ref, second_ref, first_send_ref, second_send_ref, own_product_ref, product_ref, sems = (
        refs[amount + 1 :]
    )
    me, group = me_ref[0], group_ref[0]
    copies = []

    def add(condition, source, target):
        copies.append((condition, pltpu.make_async_copy(source, target, sems.at[len(copies)])))

    for h in range(own_ref.shape[0]):
        for mask, piece in enumerate(pieces):
            other = (other_ref[h] ^ me) == mask
            add(other, piece.at[pl.ds(half, extra), :], second_send_ref.at[h])
            add(other, piece.at[pl.ds(0, half), :], first_send_ref.at[h])
            ours = (own_ref[h] ^ me) == mask
            add(ours, piece.at[pl.ds(half, extra), :], second_ref.at[h])
            start = pl.multiple_of(group * half, half)
            add(ours, piece.at[pl.ds(0, half), :], first_ref.at[h, pl.ds(start, half), :])
    for condition, copy in copies:
        pl.when(condition)(copy.start)
    mine = product_ref.shape[0]
    total = jnp.zeros((2 * mine, product_ref.shape[1]), jnp.float32)
    for mask, piece in enumerate(pieces):
        product = jnp.dot(
            tokens_ref[...], piece[pl.ds(0, half), :], preferred_element_type=jnp.float32
        )
        total = total + jnp.where(ids_ref[...] == (me ^ mask), product, 0.0)
    own_product_ref[...] = total[:mine]
    product_ref[...] = total[mine:]
    for condition, copy in copies:
        pl.when(condition)(copy.wait)


def adapt(me, group, placement, other_placement, ids, tokens, pieces, half, extra, after):
    hot = placement.shape[0]
    rank2 = pieces[0].shape[1]
    dtype = pieces[0].dtype
    return pl.pallas_call(
        functools.partial(adapt_kernel, half, extra, len(pieces)),
        out_shape=[
            jax.ShapeDtypeStruct((hot, 2 * half, rank2), dtype),
            jax.ShapeDtypeStruct((hot, extra, rank2), dtype),
            jax.ShapeDtypeStruct((hot, half, rank2), dtype),
            jax.ShapeDtypeStruct((hot, extra, rank2), dtype),
        ]
        + [jax.ShapeDtypeStruct((tokens.shape[0] // 2, rank2), jnp.float32)] * 2,
        in_specs=[SMEM] * 4 + [VMEM] * (2 + len(pieces)) + [HBM],
        out_specs=[HBM] * 4 + [VMEM] * 2,
        scratch_shapes=[pltpu.SemaphoreType.DMA((4 * hot * len(pieces),))],
        compiler_params=pltpu.CompilerParams(vmem_limit_bytes=60 << 20),
        cost_estimate=CHEAP,
        name="adapt",
    )(me, placement, other_placement, group, ids, tokens, *pieces, after)


def place_kernel(group_ref, received_ref, _, after_ref, out_ref, sem):
    half = received_ref.shape[1]
    start = pl.multiple_of((1 - group_ref[0]) * half, half)
    copy = pltpu.make_async_copy(received_ref, out_ref.at[:, pl.ds(start, half), :], sem)
    copy.start()
    copy.wait()


def place_half(group, received, out, after):
    return pl.pallas_call(
        place_kernel,
        out_shape=jax.ShapeDtypeStruct(out.shape, out.dtype),
        in_specs=[SMEM, VMEM, HBM, HBM],
        out_specs=HBM,
        scratch_shapes=[pltpu.SemaphoreType.DMA],
        compiler_params=pltpu.CompilerParams(vmem_limit_bytes=60 << 20),
        input_output_aliases={2: 0},
        cost_estimate=CHEAP,
        name="place_half",
    )(group, received, out, after)


def attend_kernel(
    place_ref, count_ref, hot_ref, group_ref, low_ref, low_other_ref, ours_ref, theirs_ref, base_ref,
    cos_ref, sin_ref, query_ref, cache_ref, out_ref, second_ref,
):
    step = cache_ref.shape[0]
    second_ref[group_ref[0]] = ours_ref[...]
    second_ref[1 - group_ref[0]] = theirs_ref[...]
    lows = (low_ref[...] + low_other_ref[...]).astype(jnp.bfloat16)
    for i in range(step):
        r = pl.program_id(0) * step + i
        start = count_ref[r] * BLOCK
        entry = hot_ref[r]
        rank = second_ref.shape[2]
        width = cache_ref.shape[3]
        context = cache_ref.shape[2]
        heads = width // LANES
        low = lows[2 * i : 2 * i + 2]
        base = base_ref[i]
        delta_key = jnp.dot(low[:, :rank], second_ref[0, entry], preferred_element_type=jnp.float32)
        delta_value = jnp.dot(low[:, rank:], second_ref[1, entry], preferred_element_type=jnp.float32)
        key_pre = base[:, :width] + delta_key
        new_value = (base[:, width:] + delta_value).astype(jnp.bfloat16)
        columns = lax.broadcasted_iota(jnp.int32, (TILE, context), 1)
        second_token = lax.broadcasted_iota(jnp.int32, (TILE, 1), 0) >= TILE // 2
        fresh_keys, fresh_values = [], []
        for head in range(heads):
            lanes = slice(head * LANES, (head + 1) * LANES)
            k = key_pre[:, lanes]
            swapped = pltpu.roll(k, LANES // 2, 1)
            new_key = (k * cos_ref[i] + swapped * sin_ref[i]).astype(jnp.bfloat16).astype(jnp.float32)
            value_rows = new_value[:, lanes].astype(jnp.float32)
            fresh_keys.append(new_key)
            fresh_values.append(value_rows)
            q = query_ref[i, head]
            qf = q.astype(jnp.float32)
            scale = HEAD_WIDTH ** (-0.5)
            scores = lax.dot_general(
                q, cache_ref[i, 0, :, lanes], (((1,), (1,)), ((), ())),
                preferred_element_type=jnp.float32,
            ) * scale
            scores = jnp.where(columns < start, scores, -1e30)
            s0 = jnp.sum(qf * new_key[0:1], -1, keepdims=True) * scale
            s1 = jnp.sum(qf * new_key[1:2], -1, keepdims=True) * scale
            s1 = jnp.where(second_token, s1, -1e30)
            top = jnp.maximum(jnp.max(scores, -1, keepdims=True), jnp.maximum(s0, s1))
            weights = jnp.exp(scores - top)
            w0 = jnp.exp(s0 - top)
            w1 = jnp.exp(s1 - top)
            total = jnp.sum(weights, -1, keepdims=True) + w0 + w1
            probs = (weights / total).astype(jnp.bfloat16)
            p0 = (w0 / total).astype(jnp.bfloat16).astype(jnp.float32)
            p1 = (w1 / total).astype(jnp.bfloat16).astype(jnp.float32)
            attended = jnp.dot(
                probs, cache_ref[i, 1, :, lanes], preferred_element_type=jnp.float32
            )
            attended = attended + p0 * value_rows[0:1] + p1 * value_rows[1:2]
            shared = TILE // 2
            for j in range(shared):
                both_tokens = jnp.concatenate(
                    [attended[j : j + 1], attended[shared + j : shared + j + 1]], 0
                )
                columns_to = pl.ds((head * shared + j) * LANES, LANES)
                out_ref[place_ref[r], :, columns_to] = both_tokens.astype(jnp.bfloat16)
        fresh = jnp.concatenate(fresh_keys + fresh_values, 1)
        out_ref[place_ref[r], :, shared * width :] = fresh.astype(jnp.bfloat16)


def attend(
    place, counts, hot, group, lows, ours, theirs, base, cos, sin, query, cache, slots
):
    requests, _, context, width = cache.shape
    heads = width // LANES

    step = math.gcd(requests, 4)

    def by_request(shape):
        return pl.BlockSpec((step,) + shape, lambda r, *_: (r,) + (0,) * len(shape))

    return pl.pallas_call(
        attend_kernel,
        out_shape=jax.ShapeDtypeStruct((slots, 2, (TILE // 2 + 2) * width), cache.dtype),
        grid_spec=pltpu.PrefetchScalarGridSpec(
            num_scalar_prefetch=4,
            grid=(requests // step,),
            in_specs=[
                pl.BlockSpec((2 * step, lows[0].shape[1]), lambda r, *_: (r, 0)),
                pl.BlockSpec((2 * step, lows[0].shape[1]), lambda r, *_: (r, 0)),
                pl.BlockSpec(ours.shape, lambda r, *_: (0, 0, 0)),
                pl.BlockSpec(ours.shape, lambda r, *_: (0, 0, 0)),
                by_request((2, 2 * width)),
                by_request((2, LANES)),
                by_request((2, LANES)),
                by_request((heads, TILE, LANES)),
                by_request((2, context, width)),
            ],
            out_specs=pl.BlockSpec(
                (slots, 2, (TILE // 2 + 2) * width), lambda r, *_: (0, 0, 0)
            ),
            scratch_shapes=[pltpu.VMEM((2,) + ours.shape, cache.dtype)],
        ),
        cost_estimate=CHEAP,
        name="attend",
    )(place, counts, hot, group, *lows, ours, theirs, base, cos, sin, query, cache)


def per_device(
    hidden,
    queries,
    earlier_token_cache,
    lengths,
    request_hot_entry,
    destination,
    placement,
    base_key_value_weight,
    adapter_first_factors,
    adapter_second_factors,
):
    replicas = lax.axis_size("replica")
    tensor = lax.axis_size("tensor")
    replica = lax.axis_index("replica").astype(jnp.int32)
    group = lax.axis_index("groups").astype(jnp.int32)
    part = lax.axis_index("tensor").astype(jnp.int32)
    requests = hidden.shape[0]
    pairs = max(1, requests // replicas)
    context, width = earlier_token_cache.shape[2:]
    heads = width // LANES
    live = context // BLOCK - 1
    piece = adapter_first_factors.shape[1]
    half = piece // 2
    rank2 = adapter_first_factors.shape[2]
    rank = rank2 // 2
    hot = placement.shape[0]
    me = replica[None]
    group_at = group[None]
    counts = lengths.reshape(-1)

    first_half = lax.dynamic_slice_in_dim(adapter_first_factors[0], group * half, half, 0)
    second_half = lax.dynamic_index_in_dim(
        adapter_second_factors[0], group, 0, keepdims=False
    ).reshape(-1, rank2)
    extra = second_half.shape[0]
    info = jnp.concatenate([counts, destination]).astype(jnp.bfloat16)
    info = jnp.pad(info[None], ((0, TILE - 1), (0, rank2 - info.shape[0])))
    pieces = {0: jnp.concatenate([first_half, second_half, info], 0)}
    bit = replicas // 2
    while bit:
        for mask in list(pieces):
            pieces[mask ^ bit] = exchange(pieces[mask], "replica", bit)
        bit //= 2
    pieces = [pieces[mask] for mask in range(replicas)]
    infos = jnp.stack([p[half + extra, : 2 * requests] for p in pieces]).astype(jnp.int32)
    count_all, dest_all = infos[:, :requests], infos[:, requests:]

    cap = live * pairs
    patterns = tuple(range(1, replicas))
    layout = tuple((p, 0, cap) for p in patterns)
    *packed, mark = pack(me, destination, counts, earlier_token_cache, layout)
    packed = dict(zip(layout, packed))

    tokens = hidden.reshape(requests * 2, -1)
    ids = jnp.repeat(placement[request_hot_entry], 2)
    notes = jnp.concatenate(
        [ids[:, None], jnp.broadcast_to(placement[None], (requests * 2, hot))], 1
    ).astype(jnp.bfloat16)
    notes = jnp.pad(notes, ((0, 0), (0, LANES - 1 - hot)))
    theirs = lax.dynamic_slice_in_dim(tokens, part * piece + (1 - group) * half, half, 1)
    (theirs,) = gate([jnp.concatenate([theirs, notes], 1)], mark)
    theirs = exchange(theirs, "groups", 1)
    other_ids = theirs[:, half].astype(jnp.int32)
    other_placement = theirs[0, half + 1 : half + 1 + hot].astype(jnp.int32)
    ours = lax.dynamic_slice_in_dim(tokens, part * piece + group * half, half, 1)
    both = jnp.concatenate([ours, theirs[:, :half]], 0)
    both_ids = jnp.broadcast_to(
        jnp.concatenate([ids, other_ids])[:, None], (4 * requests, rank2)
    )
    base = jnp.einsum(
        "ntd,dkc->ntkc", hidden, base_key_value_weight, preferred_element_type=jnp.float32
    ).reshape(requests, 2, 2 * width)
    received = {}
    first_parts = layout[1:] if len(layout) > 1 else layout
    near = layout[0]
    ready = gate(
        [packed[part] for part in first_parts],
        pieces[replicas // 2], pieces[1], both, both_ids, base,
    )
    for part, values in zip(first_parts, ready):
        received[part] = exchange(values, "replica", part[0])
    always = counts[0] > 0

    positions = (BLOCK * counts)[:, None] + jnp.arange(2)[None, :]
    half_size = HEAD_WIDTH // 2
    frequency = 10000.0 ** (-(jnp.arange(half_size, dtype=jnp.float32) * 2.0 / HEAD_WIDTH))
    angles = positions.astype(jnp.float32)[..., None] * frequency
    cos, sin = jnp.cos(angles), jnp.sin(angles)
    cos = jnp.concatenate([cos, cos], -1)
    sin = jnp.concatenate([-sin, sin], -1)
    group_size = queries.shape[2] // width
    query = (
        queries.reshape(requests, 2, heads, group_size, HEAD_WIDTH)
        .transpose(0, 2, 1, 3, 4)
        .reshape(requests, heads, 2 * group_size, HEAD_WIDTH)
    )
    (late_destination,) = gate([destination], mark)
    order = jnp.arange(requests)
    same = late_destination[:, None] == late_destination[None, :]
    arrival = jnp.sum((same & (order[None, :] < order[:, None])).astype(jnp.int32), 1)
    place = late_destination * pairs + arrival
    slots = replicas * pairs
    place, query, other_placement, cos, sin = gate([place, query, other_placement, cos, sin], mark)

    def serve():
        first, second, first_send, second_send, low, products = adapt(
            me, group_at, placement, other_placement, both_ids, both, pieces, half, extra, both
        )
        low = low + exchange(products, "groups", 1)
        second_other = exchange(second_send, "groups", 1)
        first_send, close = gate([first_send, packed[near]], low, second_other)
        close = exchange(close, "replica", 1)
        first_other = exchange(first_send, "groups", 1)
        theirs = second_other.reshape(hot, rank, width)
        bit = 1
        while 2 * bit < tensor:
            low = low + exchange(low, "tensor", bit)
            bit *= 2
        ours = second.reshape(hot, rank, width)
        lows = (low, exchange(low, "tensor", bit))
        small = attend(
            place, counts, request_hot_entry, group_at, lows, ours, theirs, base, cos, sin, query,
            earlier_token_cache, slots,
        )
        resident = jnp.where(
            group == 0, jnp.stack([ours, theirs], 1), jnp.stack([theirs, ours], 1)
        )
        smalls = lax.all_to_all(
            small.reshape((replicas, pairs) + small.shape[1:]), "replica", 0, 0, tiled=True
        )
        (out,) = unpack(
            me, dest_all, count_all, earlier_token_cache, {}, None, None, pairs, context, small
        )
        resident_first = place_half(group_at, first_other, first, out)
        (out,) = unpack(
            me, dest_all, count_all, None, {near: close}, None, out, pairs, context,
            resident_first,
        )
        return resident_first, resident, out, smalls

    def nothing():
        return (
            jnp.zeros((hot, piece, rank2), jnp.bfloat16),
            jnp.zeros((hot, 2, rank, width), jnp.bfloat16),
            jnp.zeros((slots, 2, context, width), jnp.bfloat16),
            jnp.zeros((replicas, pairs, 2, (group_size + 2) * width), jnp.bfloat16),
        )

    resident_first, resident_second, out, smalls = lax.cond(always, serve, nothing)
    moved_cache, moved_attention = unpack(
        me, dest_all, count_all, None, received, smalls, out, pairs, context, both
    )
    return (moved_cache, moved_attention, resident_first, resident_second)


def solution(mesh):
    in_specs = (
        P(("groups", "replica"), None, None),
        P(("groups", "replica"), None, "tensor"),
        P(("groups", "replica"), None, None, "tensor"),
        P(("groups", "replica"), None),
        P(("groups", "replica")),
        P(("groups", "replica")),
        P("groups"),
        P(None, None, "tensor"),
        P("replica", "tensor", None),
        P("replica", None, None, "tensor"),
    )
    out_specs = (
        P(("groups", "replica"), None, None, "tensor"),
        P(("groups", "replica"), None, "tensor"),
        P("groups", "tensor", None),
        P("groups", None, None, "tensor"),
    )
    return jax.shard_map(
        per_device, mesh=mesh, in_specs=in_specs, out_specs=out_specs, check_vma=False
    )
```

```python
import functools
import math

import jax
import jax.numpy as jnp
from jax import lax
from jax.experimental import pallas as pl
from jax.experimental.pallas import tpu as pltpu
from jax.sharding import PartitionSpec as P

HEAD_WIDTH = 128
BLOCK = 128
TILE = 16
LANES = 128
SMEM = pl.BlockSpec(memory_space=pltpu.SMEM)
VMEM = pl.BlockSpec(memory_space=pltpu.VMEM)
CHEAP = pl.CostEstimate(flops=1, bytes_accessed=1, transcendentals=0)
HBM = pl.BlockSpec(memory_space=pltpu.HBM)


def exchange(values, axis, mask):
    size = lax.axis_size(axis)
    return lax.ppermute(values, axis, [(i, i ^ mask) for i in range(size)])


def gate_kernel(*refs):
    pass


def gate(values, *after):
    return pl.pallas_call(
        gate_kernel,
        out_shape=[jax.ShapeDtypeStruct(v.shape, v.dtype) for v in values],
        in_specs=[HBM] * (len(values) + len(after)),
        out_specs=[HBM] * len(values),
        input_output_aliases={i: i for i in range(len(values))},
        cost_estimate=CHEAP,
        name="gate",
    )(*values, *after)


def pack_kernel(layout, live, me_ref, dest_ref, count_ref, cache_ref, *rest):
    outs = rest[: len(layout)]
    mark_ref, stage, in_sems, out_sems = rest[len(layout) :]
    mark_ref[...] = jnp.zeros_like(mark_ref)
    requests = dest_ref.shape[0]
    me = me_ref[0]
    moves = []
    for r in range(requests):
        blocks, target = count_ref[r], dest_ref[r]
        offset = jnp.int32(0)
        for earlier in range(r):
            offset = offset + jnp.where(dest_ref[earlier] == target, count_ref[earlier], 0)
        for b in range(live):
            index = r * live + b
            going = (b < blocks) & (target != me)
            position = offset + b
            inward = pltpu.make_async_copy(
                cache_ref.at[r, :, pl.ds(b * BLOCK, BLOCK), :], stage.at[index], in_sems.at[index]
            )
            outward = []
            for (pattern, first, amount), out_ref in zip(layout, outs):
                here = position - first
                outward.append(
                    (
                        going & (target == (me ^ pattern)) & (here >= 0) & (here < amount),
                        pltpu.make_async_copy(
                            stage.at[index],
                            out_ref.at[jnp.clip(here, 0, amount - 1)],
                            out_sems.at[index],
                        ),
                    )
                )
            moves.append((going, inward, outward))
    for going, inward, _ in moves:
        pl.when(going)(inward.start)
    for going, inward, outward in moves:
        pl.when(going)(inward.wait)
        for this, copy in outward:
            pl.when(this)(copy.start)
    for going, _, outward in moves:
        pl.when(going)(outward[0][1].wait)


def pack(me, destination, counts, cache, layout):
    requests, _, context, width = cache.shape
    live = context // BLOCK - 1
    return pl.pallas_call(
        functools.partial(pack_kernel, layout, live),
        out_shape=[
            jax.ShapeDtypeStruct((amount, 2, BLOCK, width), cache.dtype)
            for _, _, amount in layout
        ]
        + [jax.ShapeDtypeStruct((8, LANES), jnp.float32)],
        in_specs=[SMEM, SMEM, SMEM, HBM],
        out_specs=[HBM] * len(layout) + [VMEM],
        scratch_shapes=[
            pltpu.VMEM((requests * live, 2, BLOCK, width), cache.dtype),
            pltpu.SemaphoreType.DMA((requests * live,)),
            pltpu.SemaphoreType.DMA((requests * live,)),
        ],
        compiler_params=pltpu.CompilerParams(vmem_limit_bytes=60 << 20),
        cost_estimate=CHEAP,
        name="pack",
    )(me, destination, counts, cache)


def unpack_kernel(layout, own, fill, tail, pairs, live, *refs):
    me_ref, dest_ref, count_ref = refs[:3]
    at = 3
    if own:
        cache_ref = refs[at]
        at += 1
    received = refs[at : at + len(layout)]
    at += len(layout)
    replicas, requests = dest_ref.shape
    if tail:
        small_ref = refs[at]
        at += 1
    at += 1 if fill else 2
    out_ref = refs[at]
    at += 1
    if tail:
        att_ref = refs[at]
        at += 1
    sems = refs[at]
    at += 1
    if own:
        own_stage, own_sems = refs[at : at + 2]
        at += 2
    if fill:
        zero_ref = refs[at]
        at += 1
        zero_ref[...] = jnp.zeros_like(zero_ref)
    if tail:
        stage_ref = refs[at]
    width = out_ref.shape[3]
    me = me_ref[0]
    copies, moves = [], []
    used = 0

    def copy_to(source, target):
        nonlocal used
        used += 1
        return pltpu.make_async_copy(source, target, sems.at[used - 1])

    slot_info = []
    used_patterns = {of for of, _, _ in layout} | ({0} if own else set())
    for pattern in range(replicas):
        if not (fill or tail or pattern in used_patterns):
            continue
        source_replica = me ^ pattern
        arrived = jnp.int32(0)
        lengths_of = [jnp.int32(-1)] * pairs
        which = [jnp.int32(0)] * pairs
        for r in range(requests):
            mine = dest_ref[pattern, r] == me
            blocks = count_ref[pattern, r]
            for k in range(pairs):
                this = mine & (arrived == k)
                lengths_of[k] = jnp.where(this, blocks, lengths_of[k])
                which[k] = jnp.where(this, r, which[k])
            arrived = arrived + jnp.where(mine, 1, 0)
        offset = jnp.int32(0)
        for k in range(pairs):
            blocks = lengths_of[k]
            slot = source_replica * pairs + k
            for b in range(live):
                place = pl.ds(b * BLOCK, BLOCK)
                target = out_ref.at[slot, :, place, :]
                valid = b < blocks
                if pattern == 0 and own:
                    index = k * live + b
                    inward = pltpu.make_async_copy(
                        cache_ref.at[which[k], :, place, :],
                        own_stage.at[index],
                        own_sems.at[index],
                    )
                    moves.append((valid, inward, [(valid, copy_to(own_stage.at[index], target))]))
                for (of, first, amount), received_ref in zip(layout, received):
                    if of == pattern:
                        here = offset + b - first
                        source = received_ref.at[jnp.clip(here, 0, amount - 1)]
                        inside = valid & (here >= 0) & (here < amount)
                        copies.append((inside, copy_to(source, target)))
            offset = offset + jnp.maximum(blocks, 0)
            slot_info.append((pattern, k, slot, blocks))
    if fill:
        for pattern, k, slot, blocks in slot_info:
            for b in range(live + 1):
                target = out_ref.at[slot, :, pl.ds(b * BLOCK, BLOCK), :]
                copies.append((b >= blocks, copy_to(zero_ref, target)))
    for condition, inward, _ in moves:
        pl.when(condition)(inward.start)
    for condition, copy in copies:
        pl.when(condition)(copy.start)
    if tail:
        columns = att_ref.shape[2]
        for index, (pattern, k, slot, blocks) in enumerate(slot_info):
            small = small_ref[me ^ pattern, k]
            filled = blocks >= 0
            att_ref[slot] = jnp.where(filled, small[:, :columns], jnp.zeros((), small.dtype))
            fresh = small[:, columns:].astype(jnp.float32)
            for kv in range(2):
                rows = fresh[:, kv * width : (kv + 1) * width]
                rows = jnp.concatenate([rows, jnp.zeros((TILE - 2, width), jnp.float32)], 0)
                stage_ref[index, kv] = rows.astype(jnp.bfloat16)
            start = pl.multiple_of(jnp.maximum(blocks, 0) * BLOCK, BLOCK)
            copy = copy_to(stage_ref.at[index], out_ref.at[slot, :, pl.ds(start, TILE), :])
            pl.when(filled)(copy.start)
            copies.append((filled, copy))
    for condition, inward, outward in moves:
        pl.when(condition)(inward.wait)
        for going, copy in outward:
            pl.when(going)(copy.start)
            copies.append((going, copy))
    for condition, copy in copies:
        pl.when(condition)(copy.wait)


def unpack(me, dest_all, count_all, cache, received, smalls, out, pairs, context, after):
    replicas, requests = dest_all.shape
    own, fill, tail = cache is not None, out is None, smalls is not None
    layout = tuple(sorted(received))
    like = cache if own else out
    dtype, width = like.dtype, like.shape[-1]
    live = context // BLOCK - 1
    slots = replicas * pairs
    args, specs = [me, dest_all, count_all], [SMEM] * 3
    if own:
        args.append(cache)
        specs.append(HBM)
    for part in layout:
        args.append(received[part])
        specs.append(VMEM)
    if tail:
        args.append(smalls)
        specs.append(VMEM)
    aliases = {}
    if not fill:
        aliases = {len(args): 0}
        args.append(out)
        specs.append(HBM)
    args.append(after)
    specs.append(HBM)
    out_shape = [jax.ShapeDtypeStruct((slots, 2, context, width), dtype)]
    out_specs = [HBM]
    amount = (len(layout) + (1 if own else 0)) * pairs * live
    scratch = []
    if own:
        scratch.append(pltpu.VMEM((pairs * live, 2, BLOCK, width), dtype))
        scratch.append(pltpu.SemaphoreType.DMA((pairs * live,)))
    if fill:
        amount += slots * (live + 1)
        scratch.append(pltpu.VMEM((2, BLOCK, width), dtype))
    if tail:
        amount += slots
        out_shape.append(jax.ShapeDtypeStruct((slots, 2, smalls.shape[3] - 2 * width), dtype))
        out_specs.append(VMEM)
        scratch.append(pltpu.VMEM((slots, 2, TILE, width), dtype))
    return pl.pallas_call(
        functools.partial(unpack_kernel, layout, own, fill, tail, pairs, live),
        out_shape=out_shape,
        in_specs=specs,
        out_specs=out_specs,
        scratch_shapes=[pltpu.SemaphoreType.DMA((amount,))] + scratch,
        input_output_aliases=aliases,
        compiler_params=pltpu.CompilerParams(vmem_limit_bytes=60 << 20),
        cost_estimate=CHEAP,
        name="unpack",
    )(*args)


def adapt_kernel(half, extra, amount, me_ref, own_ref, other_ref, group_ref, ids_ref, tokens_ref, *refs):
    pieces = refs[:amount]
    first_ref, second_ref, first_send_ref, second_send_ref, own_product_ref, product_ref, sems = (
        refs[amount + 1 :]
    )
    me, group = me_ref[0], group_ref[0]
    copies = []

    def add(condition, source, target):
        copies.append((condition, pltpu.make_async_copy(source, target, sems.at[len(copies)])))

    for h in range(own_ref.shape[0]):
        for mask, piece in enumerate(pieces):
            other = (other_ref[h] ^ me) == mask
            add(other, piece.at[pl.ds(half, extra), :], second_send_ref.at[h])
            add(other, piece.at[pl.ds(0, half), :], first_send_ref.at[h])
            ours = (own_ref[h] ^ me) == mask
            add(ours, piece.at[pl.ds(half, extra), :], second_ref.at[h])
            start = pl.multiple_of(group * half, half)
            add(ours, piece.at[pl.ds(0, half), :], first_ref.at[h, pl.ds(start, half), :])
    for condition, copy in copies:
        pl.when(condition)(copy.start)
    mine = product_ref.shape[0]
    total = jnp.zeros((2 * mine, product_ref.shape[1]), jnp.float32)
    for mask, piece in enumerate(pieces):
        product = jnp.dot(
            tokens_ref[...], piece[pl.ds(0, half), :], preferred_element_type=jnp.float32
        )
        total = total + jnp.where(ids_ref[...] == (me ^ mask), product, 0.0)
    own_product_ref[...] = total[:mine]
    product_ref[...] = total[mine:]
    for condition, copy in copies:
        pl.when(condition)(copy.wait)


def adapt(me, group, placement, other_placement, ids, tokens, pieces, half, extra, after):
    hot = placement.shape[0]
    rank2 = pieces[0].shape[1]
    dtype = pieces[0].dtype
    return pl.pallas_call(
        functools.partial(adapt_kernel, half, extra, len(pieces)),
        out_shape=[
            jax.ShapeDtypeStruct((hot, 2 * half, rank2), dtype),
            jax.ShapeDtypeStruct((hot, extra, rank2), dtype),
            jax.ShapeDtypeStruct((hot, half, rank2), dtype),
            jax.ShapeDtypeStruct((hot, extra, rank2), dtype),
        ]
        + [jax.ShapeDtypeStruct((tokens.shape[0] // 2, rank2), jnp.float32)] * 2,
        in_specs=[SMEM] * 4 + [VMEM] * (2 + len(pieces)) + [HBM],
        out_specs=[HBM] * 4 + [VMEM] * 2,
        scratch_shapes=[pltpu.SemaphoreType.DMA((4 * hot * len(pieces),))],
        compiler_params=pltpu.CompilerParams(vmem_limit_bytes=60 << 20),
        cost_estimate=CHEAP,
        name="adapt",
    )(me, placement, other_placement, group, ids, tokens, *pieces, after)


def place_kernel(group_ref, received_ref, _, after_ref, out_ref, sem):
    half = received_ref.shape[1]
    start = pl.multiple_of((1 - group_ref[0]) * half, half)
    copy = pltpu.make_async_copy(received_ref, out_ref.at[:, pl.ds(start, half), :], sem)
    copy.start()
    copy.wait()


def place_half(group, received, out, after):
    return pl.pallas_call(
        place_kernel,
        out_shape=jax.ShapeDtypeStruct(out.shape, out.dtype),
        in_specs=[SMEM, VMEM, HBM, HBM],
        out_specs=HBM,
        scratch_shapes=[pltpu.SemaphoreType.DMA],
        compiler_params=pltpu.CompilerParams(vmem_limit_bytes=60 << 20),
        input_output_aliases={2: 0},
        cost_estimate=CHEAP,
        name="place_half",
    )(group, received, out, after)


def attend_kernel(
    place_ref, count_ref, hot_ref, group_ref, low_ref, low_other_ref, ours_ref, theirs_ref, base_ref,
    cos_ref, sin_ref, query_ref, cache_ref, out_ref, second_ref,
):
    step = cache_ref.shape[0]
    second_ref[group_ref[0]] = ours_ref[...]
    second_ref[1 - group_ref[0]] = theirs_ref[...]
    lows = (low_ref[...] + low_other_ref[...]).astype(jnp.bfloat16)
    for i in range(step):
        r = pl.program_id(0) * step + i
        start = count_ref[r] * BLOCK
        entry = hot_ref[r]
        rank = second_ref.shape[2]
        width = cache_ref.shape[3]
        context = cache_ref.shape[2]
        heads = width // LANES
        low = lows[2 * i : 2 * i + 2]
        base = base_ref[i]
        delta_key = jnp.dot(low[:, :rank], second_ref[0, entry], preferred_element_type=jnp.float32)
        delta_value = jnp.dot(low[:, rank:], second_ref[1, entry], preferred_element_type=jnp.float32)
        key_pre = base[:, :width] + delta_key
        new_value = (base[:, width:] + delta_value).astype(jnp.bfloat16)
        columns = lax.broadcasted_iota(jnp.int32, (TILE, context), 1)
        second_token = lax.broadcasted_iota(jnp.int32, (TILE, 1), 0) >= TILE // 2
        fresh_keys, fresh_values = [], []
        for head in range(heads):
            lanes = slice(head * LANES, (head + 1) * LANES)
            k = key_pre[:, lanes]
            swapped = pltpu.roll(k, LANES // 2, 1)
            new_key = (k * cos_ref[i] + swapped * sin_ref[i]).astype(jnp.bfloat16).astype(jnp.float32)
            value_rows = new_value[:, lanes].astype(jnp.float32)
            fresh_keys.append(new_key)
            fresh_values.append(value_rows)
            q = query_ref[i, head]
            qf = q.astype(jnp.float32)
            scale = HEAD_WIDTH ** (-0.5)
            scores = lax.dot_general(
                q, cache_ref[i, 0, :, lanes], (((1,), (1,)), ((), ())),
                preferred_element_type=jnp.float32,
            ) * scale
            scores = jnp.where(columns < start, scores, -1e30)
            s0 = jnp.sum(qf * new_key[0:1], -1, keepdims=True) * scale
            s1 = jnp.sum(qf * new_key[1:2], -1, keepdims=True) * scale
            s1 = jnp.where(second_token, s1, -1e30)
            top = jnp.maximum(jnp.max(scores, -1, keepdims=True), jnp.maximum(s0, s1))
            weights = jnp.exp(scores - top)
            w0 = jnp.exp(s0 - top)
            w1 = jnp.exp(s1 - top)
            total = jnp.sum(weights, -1, keepdims=True) + w0 + w1
            probs = (weights / total).astype(jnp.bfloat16)
            p0 = (w0 / total).astype(jnp.bfloat16).astype(jnp.float32)
            p1 = (w1 / total).astype(jnp.bfloat16).astype(jnp.float32)
            attended = jnp.dot(
                probs, cache_ref[i, 1, :, lanes], preferred_element_type=jnp.float32
            )
            attended = attended + p0 * value_rows[0:1] + p1 * value_rows[1:2]
            shared = TILE // 2
            for j in range(shared):
                both_tokens = jnp.concatenate(
                    [attended[j : j + 1], attended[shared + j : shared + j + 1]], 0
                )
                columns_to = pl.ds((head * shared + j) * LANES, LANES)
                out_ref[place_ref[r], :, columns_to] = both_tokens.astype(jnp.bfloat16)
        fresh = jnp.concatenate(fresh_keys + fresh_values, 1)
        out_ref[place_ref[r], :, shared * width :] = fresh.astype(jnp.bfloat16)


def attend(
    place, counts, hot, group, lows, ours, theirs, base, cos, sin, query, cache, slots
):
    requests, _, context, width = cache.shape
    heads = width // LANES

    step = math.gcd(requests, 4)

    def by_request(shape):
        return pl.BlockSpec((step,) + shape, lambda r, *_: (r,) + (0,) * len(shape))

    return pl.pallas_call(
        attend_kernel,
        out_shape=jax.ShapeDtypeStruct((slots, 2, (TILE // 2 + 2) * width), cache.dtype),
        grid_spec=pltpu.PrefetchScalarGridSpec(
            num_scalar_prefetch=4,
            grid=(requests // step,),
            in_specs=[
                pl.BlockSpec((2 * step, lows[0].shape[1]), lambda r, *_: (r, 0)),
                pl.BlockSpec((2 * step, lows[0].shape[1]), lambda r, *_: (r, 0)),
                pl.BlockSpec(ours.shape, lambda r, *_: (0, 0, 0)),
                pl.BlockSpec(ours.shape, lambda r, *_: (0, 0, 0)),
                by_request((2, 2 * width)),
                by_request((2, LANES)),
                by_request((2, LANES)),
                by_request((heads, TILE, LANES)),
                by_request((2, context, width)),
            ],
            out_specs=pl.BlockSpec(
                (slots, 2, (TILE // 2 + 2) * width), lambda r, *_: (0, 0, 0)
            ),
            scratch_shapes=[pltpu.VMEM((2,) + ours.shape, cache.dtype)],
        ),
        cost_estimate=CHEAP,
        name="attend",
    )(place, counts, hot, group, *lows, ours, theirs, base, cos, sin, query, cache)


def per_device(
    hidden,
    queries,
    earlier_token_cache,
    lengths,
    request_hot_entry,
    destination,
    placement,
    base_key_value_weight,
    adapter_first_factors,
    adapter_second_factors,
):
    replicas = lax.axis_size("replica")
    tensor = lax.axis_size("tensor")
    replica = lax.axis_index("replica").astype(jnp.int32)
    group = lax.axis_index("groups").astype(jnp.int32)
    part = lax.axis_index("tensor").astype(jnp.int32)
    requests = hidden.shape[0]
    pairs = max(1, requests // replicas)
    context, width = earlier_token_cache.shape[2:]
    heads = width // LANES
    live = context // BLOCK - 1
    piece = adapter_first_factors.shape[1]
    half = piece // 2
    rank2 = adapter_first_factors.shape[2]
    rank = rank2 // 2
    hot = placement.shape[0]
    me = replica[None]
    group_at = group[None]
    counts = lengths.reshape(-1)

    first_half = lax.dynamic_slice_in_dim(adapter_first_factors[0], group * half, half, 0)
    second_half = lax.dynamic_index_in_dim(
        adapter_second_factors[0], group, 0, keepdims=False
    ).reshape(-1, rank2)
    extra = second_half.shape[0]
    info = jnp.concatenate([counts, destination]).astype(jnp.bfloat16)
    info = jnp.pad(info[None], ((0, TILE - 1), (0, rank2 - info.shape[0])))
    pieces = {0: jnp.concatenate([first_half, second_half, info], 0)}
    bit = replicas // 2
    pieces[bit] = exchange(pieces[0], "replica", bit)
    if bit > 1:
        pieces[1] = exchange(pieces[0], "replica", 1)

    cap = live * pairs
    patterns = tuple(range(1, replicas))
    layout = tuple((p, 0, cap) for p in patterns)
    *packed, mark = pack(me, destination, counts, earlier_token_cache, layout)
    packed = dict(zip(layout, packed))

    tokens = hidden.reshape(requests * 2, -1)
    ids = jnp.repeat(placement[request_hot_entry], 2)
    notes = jnp.concatenate(
        [ids[:, None], jnp.broadcast_to(placement[None], (requests * 2, hot))], 1
    ).astype(jnp.bfloat16)
    notes = jnp.pad(notes, ((0, 0), (0, LANES - 1 - hot)))
    theirs = lax.dynamic_slice_in_dim(tokens, part * piece + (1 - group) * half, half, 1)
    (theirs,) = gate([jnp.concatenate([theirs, notes], 1)], mark)
    theirs = exchange(theirs, "groups", 1)
    other_ids = theirs[:, half].astype(jnp.int32)
    other_placement = theirs[0, half + 1 : half + 1 + hot].astype(jnp.int32)
    ours = lax.dynamic_slice_in_dim(tokens, part * piece + group * half, half, 1)
    both = jnp.concatenate([ours, theirs[:, :half]], 0)
    both_ids = jnp.broadcast_to(
        jnp.concatenate([ids, other_ids])[:, None], (4 * requests, rank2)
    )
    base = jnp.einsum(
        "ntd,dkc->ntkc", hidden, base_key_value_weight, preferred_element_type=jnp.float32
    ).reshape(requests, 2, 2 * width)
    positions = (BLOCK * counts)[:, None] + jnp.arange(2)[None, :]
    half_size = HEAD_WIDTH // 2
    frequency = 10000.0 ** (-(jnp.arange(half_size, dtype=jnp.float32) * 2.0 / HEAD_WIDTH))
    angles = positions.astype(jnp.float32)[..., None] * frequency
    cos, sin = jnp.cos(angles), jnp.sin(angles)
    cos = jnp.concatenate([cos, cos], -1)
    sin = jnp.concatenate([-sin, sin], -1)
    group_size = queries.shape[2] // width
    query = (
        queries.reshape(requests, 2, heads, group_size, HEAD_WIDTH)
        .transpose(0, 2, 1, 3, 4)
        .reshape(requests, heads, 2 * group_size, HEAD_WIDTH)
    )
    (late_destination,) = gate([destination], mark)
    order = jnp.arange(requests)
    same = late_destination[:, None] == late_destination[None, :]
    arrival = jnp.sum((same & (order[None, :] < order[:, None])).astype(jnp.int32), 1)
    place = late_destination * pairs + arrival
    slots = replicas * pairs
    place, query, other_placement, cos, sin = gate([place, query, other_placement, cos, sin], mark)

    first_bit = replicas // 2
    (pieces[first_bit],) = gate(
        [pieces[first_bit]], both, both_ids, base, place, query, other_placement, cos, sin
    )
    bit = first_bit // 2
    while bit:
        for mask in sorted(pieces):
            if mask ^ bit not in pieces:
                pieces[mask ^ bit] = exchange(pieces[mask], "replica", bit)
        bit //= 2
    pieces = [pieces[mask] for mask in range(replicas)]
    infos = jnp.stack([p[half + extra, : 2 * requests] for p in pieces]).astype(jnp.int32)
    count_all, dest_all = infos[:, :requests], infos[:, requests:]
    received = {}
    first_parts = layout[1:] if len(layout) > 1 else layout
    near = layout[0]
    ready = gate(
        [packed[part] for part in first_parts],
        pieces[first_bit], pieces[1],
    )
    for part, values in zip(first_parts, ready):
        received[part] = exchange(values, "replica", part[0])
    (ready,) = gate([packed[near]], pieces[replicas - 1])
    received[near] = exchange(ready, "replica", 1)
    always = counts[0] > 0


    def serve():
        first, second, first_send, second_send, low, products = adapt(
            me, group_at, placement, other_placement, both_ids, both, pieces, half, extra, both
        )
        low = low + exchange(products, "groups", 1)
        second_other = exchange(second_send, "groups", 1)
        (first_send,) = gate([first_send], low, second_other)
        first_other = exchange(first_send, "groups", 1)
        theirs = second_other.reshape(hot, rank, width)
        bit = 1
        while 2 * bit < tensor:
            low = low + exchange(low, "tensor", bit)
            bit *= 2
        ours = second.reshape(hot, rank, width)
        lows = (low, exchange(low, "tensor", bit))
        small = attend(
            place, counts, request_hot_entry, group_at, lows, ours, theirs, base, cos, sin, query,
            earlier_token_cache, slots,
        )
        resident = jnp.where(
            group == 0, jnp.stack([ours, theirs], 1), jnp.stack([theirs, ours], 1)
        )
        smalls = lax.all_to_all(
            small.reshape((replicas, pairs) + small.shape[1:]), "replica", 0, 0, tiled=True
        )
        (out,) = unpack(
            me, dest_all, count_all, earlier_token_cache, {}, None, None, pairs, context, small
        )
        resident_first = place_half(group_at, first_other, first, out)
        return resident_first, resident, out, smalls

    def nothing():
        return (
            jnp.zeros((hot, piece, rank2), jnp.bfloat16),
            jnp.zeros((hot, 2, rank, width), jnp.bfloat16),
            jnp.zeros((slots, 2, context, width), jnp.bfloat16),
            jnp.zeros((replicas, pairs, 2, (group_size + 2) * width), jnp.bfloat16),
        )

    resident_first, resident_second, out, smalls = lax.cond(always, serve, nothing)
    moved_cache, moved_attention = unpack(
        me, dest_all, count_all, None, received, smalls, out, pairs, context, both
    )
    return (moved_cache, moved_attention, resident_first, resident_second)


def solution(mesh):
    in_specs = (
        P(("groups", "replica"), None, None),
        P(("groups", "replica"), None, "tensor"),
        P(("groups", "replica"), None, None, "tensor"),
        P(("groups", "replica"), None),
        P(("groups", "replica")),
        P(("groups", "replica")),
        P("groups"),
        P(None, None, "tensor"),
        P("replica", "tensor", None),
        P("replica", None, None, "tensor"),
    )
    out_specs = (
        P(("groups", "replica"), None, None, "tensor"),
        P(("groups", "replica"), None, "tensor"),
        P("groups", "tensor", None),
        P("groups", None, None, "tensor"),
    )
    return jax.shard_map(
        per_device, mesh=mesh, in_specs=in_specs, out_specs=out_specs, check_vma=False
    )
```

```python
import functools
import math

import jax
import jax.numpy as jnp
from jax import lax
from jax.experimental import pallas as pl
from jax.experimental.pallas import tpu as pltpu
from jax.sharding import PartitionSpec as P

HEAD_WIDTH = 128
BLOCK = 128
TILE = 16
LANES = 128
SMEM = pl.BlockSpec(memory_space=pltpu.SMEM)
VMEM = pl.BlockSpec(memory_space=pltpu.VMEM)
CHEAP = pl.CostEstimate(flops=1, bytes_accessed=1, transcendentals=0)
HBM = pl.BlockSpec(memory_space=pltpu.HBM)


def exchange(values, axis, mask):
    size = lax.axis_size(axis)
    return lax.ppermute(values, axis, [(i, i ^ mask) for i in range(size)])


def gate_kernel(*refs):
    pass


def gate(values, *after):
    return pl.pallas_call(
        gate_kernel,
        out_shape=[jax.ShapeDtypeStruct(v.shape, v.dtype) for v in values],
        in_specs=[HBM] * (len(values) + len(after)),
        out_specs=[HBM] * len(values),
        input_output_aliases={i: i for i in range(len(values))},
        cost_estimate=CHEAP,
        name="gate",
    )(*values, *after)


def pack_kernel(layout, live, me_ref, dest_ref, count_ref, cache_ref, *rest):
    outs = rest[: len(layout)]
    mark_ref, stage, in_sems, out_sems = rest[len(layout) :]
    mark_ref[...] = jnp.zeros_like(mark_ref)
    requests = dest_ref.shape[0]
    me = me_ref[0]
    moves = []
    for r in range(requests):
        blocks, target = count_ref[r], dest_ref[r]
        offset = jnp.int32(0)
        for earlier in range(r):
            offset = offset + jnp.where(dest_ref[earlier] == target, count_ref[earlier], 0)
        for b in range(live):
            index = r * live + b
            going = (b < blocks) & (target != me)
            position = offset + b
            inward = pltpu.make_async_copy(
                cache_ref.at[r, :, pl.ds(b * BLOCK, BLOCK), :], stage.at[index], in_sems.at[index]
            )
            outward = []
            for (pattern, first, amount), out_ref in zip(layout, outs):
                here = position - first
                outward.append(
                    (
                        going & (target == (me ^ pattern)) & (here >= 0) & (here < amount),
                        pltpu.make_async_copy(
                            stage.at[index],
                            out_ref.at[jnp.clip(here, 0, amount - 1)],
                            out_sems.at[index],
                        ),
                    )
                )
            moves.append((going, inward, outward))
    for going, inward, _ in moves:
        pl.when(going)(inward.start)
    for going, inward, outward in moves:
        pl.when(going)(inward.wait)
        for this, copy in outward:
            pl.when(this)(copy.start)
    for going, _, outward in moves:
        pl.when(going)(outward[0][1].wait)


def pack(me, destination, counts, cache, layout):
    requests, _, context, width = cache.shape
    live = context // BLOCK - 1
    return pl.pallas_call(
        functools.partial(pack_kernel, layout, live),
        out_shape=[
            jax.ShapeDtypeStruct((amount, 2, BLOCK, width), cache.dtype)
            for _, _, amount in layout
        ]
        + [jax.ShapeDtypeStruct((8, LANES), jnp.float32)],
        in_specs=[SMEM, SMEM, SMEM, HBM],
        out_specs=[HBM] * len(layout) + [VMEM],
        scratch_shapes=[
            pltpu.VMEM((requests * live, 2, BLOCK, width), cache.dtype),
            pltpu.SemaphoreType.DMA((requests * live,)),
            pltpu.SemaphoreType.DMA((requests * live,)),
        ],
        compiler_params=pltpu.CompilerParams(vmem_limit_bytes=60 << 20),
        cost_estimate=CHEAP,
        name="pack",
    )(me, destination, counts, cache)


def unpack_kernel(layout, own, fill, tail, pairs, live, *refs):
    me_ref, dest_ref, count_ref = refs[:3]
    at = 3
    if own:
        cache_ref = refs[at]
        at += 1
    received = refs[at : at + len(layout)]
    at += len(layout)
    replicas, requests = dest_ref.shape
    if tail:
        small_ref = refs[at]
        at += 1
    at += 1 if fill else 2
    out_ref = refs[at]
    at += 1
    if tail:
        att_ref = refs[at]
        at += 1
    sems = refs[at]
    at += 1
    if own:
        own_stage, own_sems = refs[at : at + 2]
        at += 2
    if fill:
        zero_ref = refs[at]
        at += 1
        zero_ref[...] = jnp.zeros_like(zero_ref)
    if tail:
        stage_ref = refs[at]
    width = out_ref.shape[3]
    me = me_ref[0]
    copies, moves = [], []
    used = 0

    def copy_to(source, target):
        nonlocal used
        used += 1
        return pltpu.make_async_copy(source, target, sems.at[used - 1])

    slot_info = []
    used_patterns = {of for of, _, _ in layout} | ({0} if own else set())
    for pattern in range(replicas):
        if not (fill or tail or pattern in used_patterns):
            continue
        source_replica = me ^ pattern
        arrived = jnp.int32(0)
        lengths_of = [jnp.int32(-1)] * pairs
        which = [jnp.int32(0)] * pairs
        for r in range(requests):
            mine = dest_ref[pattern, r] == me
            blocks = count_ref[pattern, r]
            for k in range(pairs):
                this = mine & (arrived == k)
                lengths_of[k] = jnp.where(this, blocks, lengths_of[k])
                which[k] = jnp.where(this, r, which[k])
            arrived = arrived + jnp.where(mine, 1, 0)
        offset = jnp.int32(0)
        for k in range(pairs):
            blocks = lengths_of[k]
            slot = source_replica * pairs + k
            for b in range(live):
                place = pl.ds(b * BLOCK, BLOCK)
                target = out_ref.at[slot, :, place, :]
                valid = b < blocks
                if pattern == 0 and own:
                    index = k * live + b
                    inward = pltpu.make_async_copy(
                        cache_ref.at[which[k], :, place, :],
                        own_stage.at[index],
                        own_sems.at[index],
                    )
                    moves.append((valid, inward, [(valid, copy_to(own_stage.at[index], target))]))
                for (of, first, amount), received_ref in zip(layout, received):
                    if of == pattern:
                        here = offset + b - first
                        source = received_ref.at[jnp.clip(here, 0, amount - 1)]
                        inside = valid & (here >= 0) & (here < amount)
                        copies.append((inside, copy_to(source, target)))
            offset = offset + jnp.maximum(blocks, 0)
            slot_info.append((pattern, k, slot, blocks))
    if fill:
        for pattern, k, slot, blocks in slot_info:
            for b in range(live + 1):
                target = out_ref.at[slot, :, pl.ds(b * BLOCK, BLOCK), :]
                copies.append((b >= blocks, copy_to(zero_ref, target)))
    for condition, inward, _ in moves:
        pl.when(condition)(inward.start)
    for condition, copy in copies:
        pl.when(condition)(copy.start)
    if tail:
        columns = att_ref.shape[2]
        for index, (pattern, k, slot, blocks) in enumerate(slot_info):
            small = small_ref[me ^ pattern, k]
            filled = blocks >= 0
            att_ref[slot] = jnp.where(filled, small[:, :columns], jnp.zeros((), small.dtype))
            fresh = small[:, columns:].astype(jnp.float32)
            for kv in range(2):
                rows = fresh[:, kv * width : (kv + 1) * width]
                rows = jnp.concatenate([rows, jnp.zeros((TILE - 2, width), jnp.float32)], 0)
                stage_ref[index, kv] = rows.astype(jnp.bfloat16)
            start = pl.multiple_of(jnp.maximum(blocks, 0) * BLOCK, BLOCK)
            copy = copy_to(stage_ref.at[index], out_ref.at[slot, :, pl.ds(start, TILE), :])
            pl.when(filled)(copy.start)
            copies.append((filled, copy))
    for condition, inward, outward in moves:
        pl.when(condition)(inward.wait)
        for going, copy in outward:
            pl.when(going)(copy.start)
            copies.append((going, copy))
    for condition, copy in copies:
        pl.when(condition)(copy.wait)


def unpack(me, dest_all, count_all, cache, received, smalls, out, pairs, context, after):
    replicas, requests = dest_all.shape
    own, fill, tail = cache is not None, out is None, smalls is not None
    layout = tuple(sorted(received))
    like = cache if own else out
    dtype, width = like.dtype, like.shape[-1]
    live = context // BLOCK - 1
    slots = replicas * pairs
    args, specs = [me, dest_all, count_all], [SMEM] * 3
    if own:
        args.append(cache)
        specs.append(HBM)
    for part in layout:
        args.append(received[part])
        specs.append(VMEM)
    if tail:
        args.append(smalls)
        specs.append(VMEM)
    aliases = {}
    if not fill:
        aliases = {len(args): 0}
        args.append(out)
        specs.append(HBM)
    args.append(after)
    specs.append(HBM)
    out_shape = [jax.ShapeDtypeStruct((slots, 2, context, width), dtype)]
    out_specs = [HBM]
    amount = (len(layout) + (1 if own else 0)) * pairs * live
    scratch = []
    if own:
        scratch.append(pltpu.VMEM((pairs * live, 2, BLOCK, width), dtype))
        scratch.append(pltpu.SemaphoreType.DMA((pairs * live,)))
    if fill:
        amount += slots * (live + 1)
        scratch.append(pltpu.VMEM((2, BLOCK, width), dtype))
    if tail:
        amount += slots
        out_shape.append(jax.ShapeDtypeStruct((slots, 2, smalls.shape[3] - 2 * width), dtype))
        out_specs.append(VMEM)
        scratch.append(pltpu.VMEM((slots, 2, TILE, width), dtype))
    return pl.pallas_call(
        functools.partial(unpack_kernel, layout, own, fill, tail, pairs, live),
        out_shape=out_shape,
        in_specs=specs,
        out_specs=out_specs,
        scratch_shapes=[pltpu.SemaphoreType.DMA((amount,))] + scratch,
        input_output_aliases=aliases,
        compiler_params=pltpu.CompilerParams(vmem_limit_bytes=8 << 20),
        cost_estimate=CHEAP,
        name="unpack",
    )(*args)


def adapt_kernel(half, extra, amount, me_ref, own_ref, other_ref, group_ref, ids_ref, tokens_ref, *refs):
    pieces = refs[:amount]
    first_ref, second_ref, first_send_ref, second_send_ref, own_product_ref, product_ref, sems = (
        refs[amount + 1 :]
    )
    me, group = me_ref[0], group_ref[0]
    copies = []

    def add(condition, source, target):
        copies.append((condition, pltpu.make_async_copy(source, target, sems.at[len(copies)])))

    for h in range(own_ref.shape[0]):
        for mask, piece in enumerate(pieces):
            other = (other_ref[h] ^ me) == mask
            add(other, piece.at[pl.ds(half, extra), :], second_send_ref.at[h])
            add(other, piece.at[pl.ds(0, half), :], first_send_ref.at[h])
            ours = (own_ref[h] ^ me) == mask
            add(ours, piece.at[pl.ds(half, extra), :], second_ref.at[h])
            start = pl.multiple_of(group * half, half)
            add(ours, piece.at[pl.ds(0, half), :], first_ref.at[h, pl.ds(start, half), :])
    for condition, copy in copies:
        pl.when(condition)(copy.start)
    mine = product_ref.shape[0]
    total = jnp.zeros((2 * mine, product_ref.shape[1]), jnp.float32)
    for mask, piece in enumerate(pieces):
        product = jnp.dot(
            tokens_ref[...], piece[pl.ds(0, half), :], preferred_element_type=jnp.float32
        )
        total = total + jnp.where(ids_ref[...] == (me ^ mask), product, 0.0)
    own_product_ref[...] = total[:mine]
    product_ref[...] = total[mine:]
    for condition, copy in copies:
        pl.when(condition)(copy.wait)


def adapt(me, group, placement, other_placement, ids, tokens, pieces, half, extra, after):
    hot = placement.shape[0]
    rank2 = pieces[0].shape[1]
    dtype = pieces[0].dtype
    return pl.pallas_call(
        functools.partial(adapt_kernel, half, extra, len(pieces)),
        out_shape=[
            jax.ShapeDtypeStruct((hot, 2 * half, rank2), dtype),
            jax.ShapeDtypeStruct((hot, extra, rank2), dtype),
            jax.ShapeDtypeStruct((hot, half, rank2), dtype),
            jax.ShapeDtypeStruct((hot, extra, rank2), dtype),
        ]
        + [jax.ShapeDtypeStruct((tokens.shape[0] // 2, rank2), jnp.float32)] * 2,
        in_specs=[SMEM] * 4 + [VMEM] * (2 + len(pieces)) + [HBM],
        out_specs=[HBM] * 4 + [VMEM] * 2,
        scratch_shapes=[pltpu.SemaphoreType.DMA((4 * hot * len(pieces),))],
        compiler_params=pltpu.CompilerParams(vmem_limit_bytes=60 << 20),
        cost_estimate=CHEAP,
        name="adapt",
    )(me, placement, other_placement, group, ids, tokens, *pieces, after)


def place_kernel(group_ref, received_ref, _, after_ref, out_ref, sem):
    half = received_ref.shape[1]
    start = pl.multiple_of((1 - group_ref[0]) * half, half)
    copy = pltpu.make_async_copy(received_ref, out_ref.at[:, pl.ds(start, half), :], sem)
    copy.start()
    copy.wait()


def place_half(group, received, out, after):
    return pl.pallas_call(
        place_kernel,
        out_shape=jax.ShapeDtypeStruct(out.shape, out.dtype),
        in_specs=[SMEM, VMEM, HBM, HBM],
        out_specs=HBM,
        scratch_shapes=[pltpu.SemaphoreType.DMA],
        compiler_params=pltpu.CompilerParams(vmem_limit_bytes=8 << 20),
        input_output_aliases={2: 0},
        cost_estimate=CHEAP,
        name="place_half",
    )(group, received, out, after)


def attend_kernel(
    place_ref, count_ref, hot_ref, group_ref, low_ref, low_other_ref, ours_ref, theirs_ref, base_ref,
    cos_ref, sin_ref, query_ref, cache_ref, out_ref, second_ref,
):
    step = cache_ref.shape[0]
    second_ref[group_ref[0]] = ours_ref[...]
    second_ref[1 - group_ref[0]] = theirs_ref[...]
    lows = (low_ref[...] + low_other_ref[...]).astype(jnp.bfloat16)
    for i in range(step):
        r = pl.program_id(0) * step + i
        start = count_ref[r] * BLOCK
        entry = hot_ref[r]
        rank = second_ref.shape[2]
        width = cache_ref.shape[3]
        context = cache_ref.shape[2]
        heads = width // LANES
        low = lows[2 * i : 2 * i + 2]
        base = base_ref[i]
        delta_key = jnp.dot(low[:, :rank], second_ref[0, entry], preferred_element_type=jnp.float32)
        delta_value = jnp.dot(low[:, rank:], second_ref[1, entry], preferred_element_type=jnp.float32)
        key_pre = base[:, :width] + delta_key
        new_value = (base[:, width:] + delta_value).astype(jnp.bfloat16)
        columns = lax.broadcasted_iota(jnp.int32, (TILE, context), 1)
        second_token = lax.broadcasted_iota(jnp.int32, (TILE, 1), 0) >= TILE // 2
        fresh_keys, fresh_values = [], []
        for head in range(heads):
            lanes = slice(head * LANES, (head + 1) * LANES)
            k = key_pre[:, lanes]
            swapped = pltpu.roll(k, LANES // 2, 1)
            new_key = (k * cos_ref[i] + swapped * sin_ref[i]).astype(jnp.bfloat16).astype(jnp.float32)
            value_rows = new_value[:, lanes].astype(jnp.float32)
            fresh_keys.append(new_key)
            fresh_values.append(value_rows)
            q = query_ref[i, head]
            qf = q.astype(jnp.float32)
            scale = HEAD_WIDTH ** (-0.5)
            scores = lax.dot_general(
                q, cache_ref[i, 0, :, lanes], (((1,), (1,)), ((), ())),
                preferred_element_type=jnp.float32,
            ) * scale
            scores = jnp.where(columns < start, scores, -1e30)
            s0 = jnp.sum(qf * new_key[0:1], -1, keepdims=True) * scale
            s1 = jnp.sum(qf * new_key[1:2], -1, keepdims=True) * scale
            s1 = jnp.where(second_token, s1, -1e30)
            top = jnp.maximum(jnp.max(scores, -1, keepdims=True), jnp.maximum(s0, s1))
            weights = jnp.exp(scores - top)
            w0 = jnp.exp(s0 - top)
            w1 = jnp.exp(s1 - top)
            total = jnp.sum(weights, -1, keepdims=True) + w0 + w1
            probs = (weights / total).astype(jnp.bfloat16)
            p0 = (w0 / total).astype(jnp.bfloat16).astype(jnp.float32)
            p1 = (w1 / total).astype(jnp.bfloat16).astype(jnp.float32)
            attended = jnp.dot(
                probs, cache_ref[i, 1, :, lanes], preferred_element_type=jnp.float32
            )
            attended = attended + p0 * value_rows[0:1] + p1 * value_rows[1:2]
            shared = TILE // 2
            for j in range(shared):
                both_tokens = jnp.concatenate(
                    [attended[j : j + 1], attended[shared + j : shared + j + 1]], 0
                )
                columns_to = pl.ds((head * shared + j) * LANES, LANES)
                out_ref[place_ref[r], :, columns_to] = both_tokens.astype(jnp.bfloat16)
        fresh = jnp.concatenate(fresh_keys + fresh_values, 1)
        out_ref[place_ref[r], :, shared * width :] = fresh.astype(jnp.bfloat16)


def attend(
    place, counts, hot, group, lows, ours, theirs, base, cos, sin, query, cache, slots
):
    requests, _, context, width = cache.shape
    heads = width // LANES

    step = math.gcd(requests, 4)

    def by_request(shape):
        return pl.BlockSpec((step,) + shape, lambda r, *_: (r,) + (0,) * len(shape))

    return pl.pallas_call(
        attend_kernel,
        out_shape=jax.ShapeDtypeStruct((slots, 2, (TILE // 2 + 2) * width), cache.dtype),
        grid_spec=pltpu.PrefetchScalarGridSpec(
            num_scalar_prefetch=4,
            grid=(requests // step,),
            in_specs=[
                pl.BlockSpec((2 * step, lows[0].shape[1]), lambda r, *_: (r, 0)),
                pl.BlockSpec((2 * step, lows[0].shape[1]), lambda r, *_: (r, 0)),
                pl.BlockSpec(ours.shape, lambda r, *_: (0, 0, 0)),
                pl.BlockSpec(ours.shape, lambda r, *_: (0, 0, 0)),
                by_request((2, 2 * width)),
                by_request((2, LANES)),
                by_request((2, LANES)),
                by_request((heads, TILE, LANES)),
                by_request((2, context, width)),
            ],
            out_specs=pl.BlockSpec(
                (slots, 2, (TILE // 2 + 2) * width), lambda r, *_: (0, 0, 0)
            ),
            scratch_shapes=[pltpu.VMEM((2,) + ours.shape, cache.dtype)],
        ),
        cost_estimate=CHEAP,
        name="attend",
    )(place, counts, hot, group, *lows, ours, theirs, base, cos, sin, query, cache)


def per_device(
    hidden,
    queries,
    earlier_token_cache,
    lengths,
    request_hot_entry,
    destination,
    placement,
    base_key_value_weight,
    adapter_first_factors,
    adapter_second_factors,
):
    replicas = lax.axis_size("replica")
    tensor = lax.axis_size("tensor")
    replica = lax.axis_index("replica").astype(jnp.int32)
    group = lax.axis_index("groups").astype(jnp.int32)
    part = lax.axis_index("tensor").astype(jnp.int32)
    requests = hidden.shape[0]
    pairs = max(1, requests // replicas)
    context, width = earlier_token_cache.shape[2:]
    heads = width // LANES
    live = context // BLOCK - 1
    piece = adapter_first_factors.shape[1]
    half = piece // 2
    rank2 = adapter_first_factors.shape[2]
    rank = rank2 // 2
    hot = placement.shape[0]
    me = replica[None]
    group_at = group[None]
    counts = lengths.reshape(-1)

    first_half = lax.dynamic_slice_in_dim(adapter_first_factors[0], group * half, half, 0)
    second_half = lax.dynamic_index_in_dim(
        adapter_second_factors[0], group, 0, keepdims=False
    ).reshape(-1, rank2)
    extra = second_half.shape[0]
    info = jnp.concatenate([counts, destination]).astype(jnp.bfloat16)
    info = jnp.pad(info[None], ((0, TILE - 1), (0, rank2 - info.shape[0])))
    pieces = {0: jnp.concatenate([first_half, second_half, info], 0)}
    bit = replicas // 2
    pieces[bit] = exchange(pieces[0], "replica", bit)
    if bit > 1:
        pieces[1] = exchange(pieces[0], "replica", 1)

    cap = live * pairs
    patterns = tuple(range(1, replicas))
    layout = tuple((p, 0, cap) for p in patterns)
    *packed, mark = pack(me, destination, counts, earlier_token_cache, layout)
    packed = dict(zip(layout, packed))

    tokens = hidden.reshape(requests * 2, -1)
    ids = jnp.repeat(placement[request_hot_entry], 2)
    notes = jnp.concatenate(
        [ids[:, None], jnp.broadcast_to(placement[None], (requests * 2, hot))], 1
    ).astype(jnp.bfloat16)
    notes = jnp.pad(notes, ((0, 0), (0, LANES - 1 - hot)))
    theirs = lax.dynamic_slice_in_dim(tokens, part * piece + (1 - group) * half, half, 1)
    (theirs,) = gate([jnp.concatenate([theirs, notes], 1)], mark)
    theirs = exchange(theirs, "groups", 1)
    other_ids = theirs[:, half].astype(jnp.int32)
    other_placement = theirs[0, half + 1 : half + 1 + hot].astype(jnp.int32)
    ours = lax.dynamic_slice_in_dim(tokens, part * piece + group * half, half, 1)
    both = jnp.concatenate([ours, theirs[:, :half]], 0)
    both_ids = jnp.broadcast_to(
        jnp.concatenate([ids, other_ids])[:, None], (4 * requests, rank2)
    )
    base = jnp.einsum(
        "ntd,dkc->ntkc", hidden, base_key_value_weight, preferred_element_type=jnp.float32
    ).reshape(requests, 2, 2 * width)
    positions = (BLOCK * counts)[:, None] + jnp.arange(2)[None, :]
    half_size = HEAD_WIDTH // 2
    frequency = 10000.0 ** (-(jnp.arange(half_size, dtype=jnp.float32) * 2.0 / HEAD_WIDTH))
    angles = positions.astype(jnp.float32)[..., None] * frequency
    cos, sin = jnp.cos(angles), jnp.sin(angles)
    cos = jnp.concatenate([cos, cos], -1)
    sin = jnp.concatenate([-sin, sin], -1)
    group_size = queries.shape[2] // width
    query = (
        queries.reshape(requests, 2, heads, group_size, HEAD_WIDTH)
        .transpose(0, 2, 1, 3, 4)
        .reshape(requests, heads, 2 * group_size, HEAD_WIDTH)
    )
    (late_destination,) = gate([destination], mark)
    order = jnp.arange(requests)
    same = late_destination[:, None] == late_destination[None, :]
    arrival = jnp.sum((same & (order[None, :] < order[:, None])).astype(jnp.int32), 1)
    place = late_destination * pairs + arrival
    slots = replicas * pairs
    place, query, other_placement, cos, sin = gate([place, query, other_placement, cos, sin], mark)

    first_bit = replicas // 2
    (pieces[first_bit],) = gate(
        [pieces[first_bit]], both, both_ids, base, place, query, other_placement, cos, sin
    )
    bit = first_bit // 2
    while bit:
        for mask in sorted(pieces):
            if mask ^ bit not in pieces:
                pieces[mask ^ bit] = exchange(pieces[mask], "replica", bit)
        bit //= 2
    pieces = [pieces[mask] for mask in range(replicas)]
    infos = jnp.stack([p[half + extra, : 2 * requests] for p in pieces]).astype(jnp.int32)
    count_all, dest_all = infos[:, :requests], infos[:, requests:]
    received = {}
    first_parts = layout[1:] if len(layout) > 1 else layout
    near = layout[0]
    ready = gate(
        [packed[part] for part in first_parts],
        pieces[first_bit], pieces[1],
    )
    for part, values in zip(first_parts, ready):
        received[part] = exchange(values, "replica", part[0])
    (ready,) = gate([packed[near]], pieces[replicas - 1])
    received[near] = exchange(ready, "replica", 1)
    always = counts[0] > 0


    def serve():
        first, second, first_send, second_send, low, products = adapt(
            me, group_at, placement, other_placement, both_ids, both, pieces, half, extra, both
        )
        low = low + exchange(products, "groups", 1)
        second_other = exchange(second_send, "groups", 1)
        (first_send,) = gate([first_send], low, second_other)
        first_other = exchange(first_send, "groups", 1)
        theirs = second_other.reshape(hot, rank, width)
        bit = 1
        while 2 * bit < tensor:
            low = low + exchange(low, "tensor", bit)
            bit *= 2
        ours = second.reshape(hot, rank, width)
        lows = (low, exchange(low, "tensor", bit))
        small = attend(
            place, counts, request_hot_entry, group_at, lows, ours, theirs, base, cos, sin, query,
            earlier_token_cache, slots,
        )
        resident = jnp.where(
            group == 0, jnp.stack([ours, theirs], 1), jnp.stack([theirs, ours], 1)
        )
        smalls = lax.all_to_all(
            small.reshape((replicas, pairs) + small.shape[1:]), "replica", 0, 0, tiled=True
        )
        (out,) = unpack(
            me, dest_all, count_all, earlier_token_cache, {}, None, None, pairs, context, small
        )
        resident_first = place_half(group_at, first_other, first, out)
        return resident_first, resident, out, smalls

    def nothing():
        return (
            jnp.zeros((hot, piece, rank2), jnp.bfloat16),
            jnp.zeros((hot, 2, rank, width), jnp.bfloat16),
            jnp.zeros((slots, 2, context, width), jnp.bfloat16),
            jnp.zeros((replicas, pairs, 2, (group_size + 2) * width), jnp.bfloat16),
        )

    resident_first, resident_second, out, smalls = lax.cond(always, serve, nothing)
    moved_cache, moved_attention = unpack(
        me, dest_all, count_all, None, received, smalls, out, pairs, context, both
    )
    return (moved_cache, moved_attention, resident_first, resident_second)


def solution(mesh):
    in_specs = (
        P(("groups", "replica"), None, None),
        P(("groups", "replica"), None, "tensor"),
        P(("groups", "replica"), None, None, "tensor"),
        P(("groups", "replica"), None),
        P(("groups", "replica")),
        P(("groups", "replica")),
        P("groups"),
        P(None, None, "tensor"),
        P("replica", "tensor", None),
        P("replica", None, None, "tensor"),
    )
    out_specs = (
        P(("groups", "replica"), None, None, "tensor"),
        P(("groups", "replica"), None, "tensor"),
        P("groups", "tensor", None),
        P("groups", None, None, "tensor"),
    )
    return jax.shard_map(
        per_device, mesh=mesh, in_specs=in_specs, out_specs=out_specs, check_vma=False
    )
```
